256 devices in a mesh: gx: 4 (over x_hi, core), gy: 16 (over z, x_lo), mz: 4 (over y).
Axes of the slice: x: 4 (x_hi: 2, x_lo: 2; x = x_hi * 2 + x_lo), y: 4, z: 8, core: 2. Of those that a mesh axis runs over, the one named last changes fastest.
Arguments:
- counts: int32 [128, 32, 256, 256], P('mz', 'gx', 'gy'), may hold values from 0 to 24
- kernel_taps: float32 [3, 5], replicated, may hold values from 0.1 to 1
- peak_bins: int32 [24, 4], replicated, may hold values from 0 to 127, as said below
- peak_share: float32 [24, 4], replicated, may hold values from 0.1 to 1
Outputs:
- abundance: float32 [24, 32, 256, 256], P(None, ('gx', 'mz'), 'gy')
The draws below stay inside these ranges and needn't reach their ends.
Inputs may be any that keep to these rules, and one draw needn't show every extreme that they name: `peak_bins`: no two isotope peaks of the same element share a bin; peaks of different elements may.
All inputs are finite; a program needn't handle non-finite values.
Results may differ from the reference program's by a relative error of at most 0.000092.
Values sent between devices are 32-bit elements; how exact they have to be, the bound alone decides.
No kernel may reach another device: no remote copies, remote signals or barrier semaphores. Data moves between devices by JAX's collectives and lax.ppermute only.
A program may use at most 64 MiB of HBM per device.

```python
import jax
import jax.numpy as jnp
from jax import lax

NB = 128
NE = 24
NI = 4
NZ = 256
NX = 32
NY = 256


def draw_counts(key, part):
    level_key = jax.random.fold_in(key, 11)
    value_key = jax.random.fold_in(key, 12)
    levels = jax.random.permutation(level_key, NB) % 6
    x_index = jnp.arange(NX, dtype=jnp.int32)
    y_index = jnp.arange(NY, dtype=jnp.int32)
    ceiling = 2 + levels[:, None, None, None] + (16 * y_index // NY)[None, None, :, None] + (4 * x_index // NX)[None, :, None, None]
    ceiling = jnp.broadcast_to(ceiling, (NB, NX, NY, NZ))
    return jax.random.randint(value_key, (NB, NX, NY, NZ), 0, ceiling, dtype=jnp.int32)


def draw_peak_bins(key, part):
    order_key = jax.random.fold_in(key, 21)
    chosen = jax.random.permutation(order_key, jnp.arange(NB, dtype=jnp.int32))
    return chosen[:NE * NI].reshape(NE, NI).astype(jnp.int32)


def setup_inputs(seed: int = 0) -> dict:
    splits = jax.random.split(jax.random.key(seed), 5)
    return {
        "counts": draw_counts(jax.random.fold_in(splits[4], 71), 0),
        "kernel_taps": jnp.clip(jax.random.uniform(splits[1], (3, 5), jnp.float32, 0.1, 1.0), 0.1, 1.0),
        "peak_bins": draw_peak_bins(jax.random.fold_in(splits[4], 71), 0),
        "peak_share": jnp.clip(jax.random.uniform(splits[3], (NE, NI), jnp.float32, 0.1, 1.0), 0.1, 1.0),
    }


RIDGE_WEIGHT = 0.5

def pad_axis(values, along):
    widths = [(0, 0)] * values.ndim
    widths[along] = (2, 2)
    return jnp.pad(values, widths)

def run_taps(padded, weights, along, length):
    summed = weights[0] * lax.slice_in_dim(padded, 0, length, axis=along)
    for offset in range(1, 5):
        summed = summed + weights[offset] * lax.slice_in_dim(padded, offset, offset + length, axis=along)
    return summed

def coordinate(positions, extent):
    return (2.0 * positions.astype(jnp.float32) + 1.0) / float(extent) - 1.0

def squares(size_x, size_y, size_z):
    full_x = coordinate(jnp.arange(size_x, dtype=jnp.int32), size_x)
    full_y = coordinate(jnp.arange(size_y, dtype=jnp.int32), size_y)
    full_z = coordinate(jnp.arange(size_z, dtype=jnp.int32), size_z)
    return jnp.stack([jnp.asarray(float(size_x * size_y * size_z), jnp.float32), jnp.sum(full_x * full_x) * float(size_y * size_z), jnp.sum(full_y * full_y) * float(size_x * size_z), jnp.sum(full_z * full_z) * float(size_x * size_y)])

def moments(values, coord_x, coord_y, coord_z):
    plane_x = jnp.sum(values, axis=(2, 3))
    plane_y = jnp.sum(values, axis=(1, 3))
    plane_z = jnp.sum(values, axis=(1, 2))
    return jnp.stack([jnp.sum(plane_x, axis=1), jnp.dot(plane_x, coord_x, precision=lax.Precision.HIGHEST), jnp.dot(plane_y, coord_y, precision=lax.Precision.HIGHEST), jnp.dot(plane_z, coord_z, precision=lax.Precision.HIGHEST)], axis=1)

def background(fitted, coord_x, coord_y, coord_z):
    return fitted[:, 0, None, None, None] + fitted[:, 1, None, None, None] * coord_x[None, :, None, None] + fitted[:, 2, None, None, None] * coord_y[None, None, :, None] + fitted[:, 3, None, None, None] * coord_z[None, None, None, :]

def unmix_matrix(peak_bins, peak_share, all_bins):
    one_hot = (peak_bins[:, :, None] == jnp.arange(all_bins, dtype=jnp.int32)[None, None, :]).astype(jnp.float32)
    mixing_t = jnp.sum(peak_share[:, :, None] * one_hot, axis=1)
    gram_matrix = jnp.dot(mixing_t.T, mixing_t, precision=lax.Precision.HIGHEST) + RIDGE_WEIGHT * jnp.eye(all_bins, dtype=jnp.float32)
    factor = jnp.linalg.cholesky(gram_matrix)
    lower_part = lax.linalg.triangular_solve(factor, mixing_t.T, left_side=True, lower=True)
    solved = lax.linalg.triangular_solve(factor, lower_part, left_side=True, lower=True, transpose_a=True)
    return solved.T

def reference(counts, kernel_taps, peak_bins, peak_share):
    weights = kernel_taps / jnp.sum(kernel_taps, axis=1, keepdims=True)
    all_bins, size_x, size_y, size_z = counts.shape

    def smooth_bin(counts_bin):
        values = counts_bin.astype(jnp.float32)
        values = run_taps(pad_axis(values, 2), weights[2], 2, size_z)
        values = run_taps(pad_axis(values, 0), weights[0], 0, size_x)
        return run_taps(pad_axis(values, 1), weights[1], 1, size_y)
    smoothed = lax.map(smooth_bin, counts)
    coord_x = coordinate(jnp.arange(size_x, dtype=jnp.int32), size_x)
    coord_y = coordinate(jnp.arange(size_y, dtype=jnp.int32), size_y)
    coord_z = coordinate(jnp.arange(size_z, dtype=jnp.int32), size_z)
    fitted = moments(smoothed, coord_x, coord_y, coord_z) / squares(size_x, size_y, size_z)[None, :]
    cleaned = smoothed - background(fitted, coord_x, coord_y, coord_z)
    unmix_rows = unmix_matrix(peak_bins, peak_share, all_bins)
    products = jnp.dot(unmix_rows, cleaned.reshape(all_bins, -1), precision=lax.Precision.HIGHEST)
    return products.reshape(unmix_rows.shape[0], size_x, size_y, size_z)
```

```python
import functools

import jax
import jax.numpy as jnp
from jax import lax
from jax.experimental import pallas as pl
from jax.experimental.pallas import tpu as pltpu
from jax.sharding import PartitionSpec as P

RIDGE_WEIGHT = 0.5
TAPS = 5
REACH = 2
LANES = 128
HIGHEST = lax.Precision.HIGHEST
VMEM_LIMIT = 48 * 1024 * 1024

GROUPS = ((tuple(range(8)), tuple(range(8, 16))),)


def iota(shape, dim):
    return lax.broadcasted_iota(jnp.int32, shape, dim)


def normalized(taps_ref):
    taps = taps_ref[...]
    return taps / jnp.sum(taps, axis=1, keepdims=True)


def tap(weights, axis, offset):
    return weights[axis : axis + 1, offset : offset + 1]


def adjoint(weights, axis, positions, extent):
    ones = jnp.zeros(positions.shape, jnp.float32)
    linear = jnp.zeros(positions.shape, jnp.float32)
    for offset in range(TAPS):
        target = positions - (offset - REACH)
        inside = (target >= 0) & (target < extent)
        weight = jnp.where(inside, tap(weights, axis, offset), 0.0)
        coordinate = (2.0 * target.astype(jnp.float32) + 1.0) / float(extent) - 1.0
        ones = ones + weight
        linear = linear + weight * coordinate
    return ones, linear


def unmix_rows(bins_ref, share_ref, all_bins):
    elements, peaks = bins_ref.shape
    bins = bins_ref[...]
    share = share_ref[...]
    lanes = iota((elements, all_bins), 1)
    mixing_t = jnp.zeros((elements, all_bins), jnp.float32)
    for peak in range(peaks):
        mixing_t = mixing_t + jnp.where(
            lanes == bins[:, peak : peak + 1], share[:, peak : peak + 1], 0.0
        )
    left = lax.dot_general(
        mixing_t, mixing_t, (((1,), (1,)), ((), ())), precision=HIGHEST,
        preferred_element_type=jnp.float32,
    )
    square = (elements, elements)
    left = left + jnp.where(iota(square, 0) == iota(square, 1), RIDGE_WEIGHT, 0.0)
    right = mixing_t
    for step in range(elements):
        inverse = 1.0 / left[step : step + 1, step : step + 1]
        left_row = left[step : step + 1, :] * inverse
        right_row = right[step : step + 1, :] * inverse
        column = left[:, step : step + 1]
        here = iota((elements, 1), 0) == step
        left = jnp.where(here, left_row, left - column * left_row)
        right = jnp.where(here, right_row, right - column * right_row)
    return right


def mix_kernel(sizes, groups, place_ref, taps_ref, bins_ref, share_ref, counts_ref, *rest):
    local_bins, local_x, local_y, depth, elements, split, all_bins, size_x, size_y, devices = sizes
    count = len(groups)
    outs, moments_ref = rest[: 3 * count], rest[3 * count]
    held, table, sums, sem = rest[3 * count + 1 :]
    rows_in = local_bins * local_x
    copies = [
        pltpu.make_async_copy(counts_ref.at[:, pl.ds(lane * LANES, LANES)], held.at[lane], sem.at[lane])
        for lane in range(depth // LANES)
    ]
    for copy in copies:
        copy.start()
    at_x, at_y, at_m = place_ref[0], place_ref[1], place_ref[2]
    weights = normalized(taps_ref)
    unmix = unmix_rows(bins_ref, share_ref, all_bins)
    expand_shape = (all_bins, rows_in)
    expand = jnp.where(
        iota(expand_shape, 0) == at_m * local_bins + iota(expand_shape, 1) // local_x, 1.0, 0.0
    )
    spread = jnp.dot(unmix, expand, precision=HIGHEST, preferred_element_type=jnp.float32)
    layer = iota((1, rows_in), 1) % local_x
    targets = []
    for ahead in range(split):
        owner = (at_m + ahead) % split
        targets += [owner * REACH + j for j in range(REACH)]
    targets += [j - REACH for j in range(REACH)] + [local_x + j for j in range(REACH)]
    for place, target in enumerate(targets):
        factor = jnp.zeros((1, rows_in), jnp.float32)
        for offset in range(TAPS):
            factor = jnp.where(layer - target + REACH == offset, tap(weights, 0, offset), factor)
        table[pl.ds(place * elements, elements), :] = spread * factor
    wide = table[...]
    high = wide.astype(jnp.bfloat16)
    low = (wide - high.astype(jnp.float32)).astype(jnp.bfloat16)
    rows_y = at_y * local_y + iota((local_y, depth), 0)
    ones_y, linear_y = adjoint(weights, 1, rows_y, size_y)
    for copy in copies:
        copy.wait()
    block = REACH * elements
    first = True
    for group, halves in enumerate(groups):
        main_ref, up_ref, down_ref = outs[3 * group : 3 * group + 3]
        for slot, row in enumerate(halves[0] + halves[1]):
            plane = jnp.concatenate(
                [
                    held[lane, pl.ds(row, rows_in, stride=local_y), :]
                    for lane in range(depth // LANES)
                ],
                axis=1,
            )
            plane = plane.astype(jnp.float32).astype(jnp.bfloat16)
            mixed = jnp.dot(high, plane, preferred_element_type=jnp.float32) + jnp.dot(
                low, plane, preferred_element_type=jnp.float32
            )
            for ahead in range(split):
                main_ref[ahead, slot] = mixed[ahead * block : (ahead + 1) * block]
            up_ref[slot] = mixed[split * block : (split + 1) * block]
            down_ref[slot] = mixed[(split + 1) * block :]
            plain = mixed * ones_y[row : row + 1, :]
            tilted = mixed * linear_y[row : row + 1, :]
            if first:
                sums[0], sums[1] = plain, tilted
                first = False
            else:
                sums[0] += plain
                sums[1] += tilted
    parts = [jnp.zeros((elements, depth), jnp.float32) for _ in range(3)]
    for place, target in enumerate(targets):
        x = at_x * local_x + target
        inside = jnp.where((x >= 0) & (x < size_x), 1.0, 0.0)
        coordinate = (2.0 * lax.convert_element_type(x, jnp.float32) + 1.0) / float(size_x) - 1.0
        rows = pl.ds(place * elements, elements)
        plain = sums[0, rows, :] * inside
        parts[0] = parts[0] + plain
        parts[1] = parts[1] + plain * coordinate
        parts[2] = parts[2] + sums[1, rows, :] * inside
    stacked = jnp.concatenate(
        [parts[0], parts[1], parts[2], parts[0], jnp.zeros((128 - 4 * elements, depth), jnp.float32)],
        axis=0,
    )
    ones_z, linear_z = adjoint(weights, 2, iota((8, depth), 1), depth)
    profile = jnp.where(iota((8, depth), 0) == 0, ones_z, linear_z)
    products = lax.dot_general(
        profile, stacked, (((1,), (1,)), ((), ())), precision=HIGHEST,
        preferred_element_type=jnp.float32,
    )
    row = jnp.where(iota((1, 128), 1) < 3 * elements, products[0:1], products[1:2])
    moments_ref[...] = jnp.broadcast_to(row, (devices, 128))


def mix(place, taps, bins, share, counts, sizes, groups):
    local_bins, local_x, local_y, depth, elements, split, _, _, _, devices = sizes
    block = REACH * elements
    shapes = []
    for halves in groups:
        length = len(halves[0]) + len(halves[1])
        shapes.append((split, length, block, depth))
        shapes += [(length, block, depth)] * 2
    shapes.append((devices, 128))
    rows_out = (split + 2) * block
    vmem = pl.BlockSpec(memory_space=pltpu.VMEM)
    return pl.pallas_call(
        functools.partial(mix_kernel, sizes, groups),
        out_shape=[jax.ShapeDtypeStruct(shape, jnp.float32) for shape in shapes],
        in_specs=[pl.BlockSpec(memory_space=pltpu.SMEM), vmem, vmem, vmem,
                  pl.BlockSpec(memory_space=pl.ANY)],
        out_specs=[vmem] * len(shapes),
        scratch_shapes=[
            pltpu.VMEM((depth // LANES, local_bins * local_x * local_y, LANES), jnp.int32),
            pltpu.VMEM((rows_out, local_bins * local_x), jnp.float32),
            pltpu.VMEM((2, rows_out, depth), jnp.float32),
            pltpu.SemaphoreType.DMA((depth // LANES,)),
        ],
        compiler_params=pltpu.CompilerParams(vmem_limit_bytes=VMEM_LIMIT),
        cost_estimate=pl.CostEstimate(
            flops=4 * rows_out * local_bins * local_x * local_y * depth,
            bytes_accessed=10 * 1024 * 1024,
            transcendentals=0,
        ),
        name="mix_bins",
    )(place, taps, bins, share, counts.reshape(-1, depth))


def finish_kernel(sizes, groups, squares, place_ref, taps_ref, moments_ref, before_ref, after_ref, *rest):
    local_y, depth, elements, split, local_x, size_x, size_y = sizes
    out_ref, turned = rest[-2:]
    block = REACH * elements
    at_x, at_y, at_m = place_ref[0], place_ref[1], place_ref[2]
    weights = normalized(taps_ref)
    planes = {}
    for j in range(REACH):
        planes[j - REACH] = before_ref[j]
        planes[local_y + j] = after_ref[j]
    for group, halves in enumerate(groups):
        refs = rest[5 * group : 5 * group + 5]
        own, near, far = refs[0], refs[1:3], refs[3:5]
        length = len(halves[0])
        for half in range(2):
            for slot, row in enumerate(halves[half]):
                planes[row] = own[half * length + slot] + near[half][slot] + far[half][slot]
    totals = jnp.sum(moments_ref[...], axis=0, keepdims=True)
    lanes = iota((elements, 128), 1)
    rows = iota((elements, 128), 0)
    fitted = [
        jnp.sum(jnp.where(lanes == rows + j * elements, totals, 0.0), axis=1, keepdims=True)
        / squares[j]
        for j in range(4)
    ]
    at = at_x * local_x + at_m * REACH
    bases = []
    for j in range(REACH):
        coordinate = (2.0 * lax.convert_element_type(at + j, jnp.float32) + 1.0) / float(size_x) - 1.0
        bases.append(fitted[0] + fitted[1] * coordinate)
    base = jnp.concatenate(bases, axis=0)
    slope_y = jnp.concatenate([fitted[2]] * REACH, axis=0)
    slope_z = jnp.concatenate([fitted[3]] * REACH, axis=0)
    line = iota((1, depth), 1)
    tilted = base + slope_z * ((2.0 * line.astype(jnp.float32) + 1.0) / float(depth) - 1.0)
    edge = []
    for offset in range(TAPS):
        source = line + (offset - REACH)
        edge.append(jnp.where((source >= 0) & (source < depth), tap(weights, 2, offset), 0.0))
    for row in range(local_y):
        smooth = tap(weights, 1, 0) * planes[row - REACH]
        for offset in range(1, TAPS):
            smooth = smooth + tap(weights, 1, offset) * planes[row + offset - REACH]
        y = at_y * local_y + row
        coordinate = (2.0 * lax.convert_element_type(y, jnp.float32) + 1.0) / float(size_y) - 1.0
        result = -(tilted + slope_y * coordinate)
        for offset in range(TAPS):
            shifted = smooth if offset == REACH else pltpu.roll(smooth, (REACH - offset) % depth, 1)
            result = result + edge[offset] * shifted
        for j in range(REACH):
            for lane in range(depth // LANES):
                turned[lane, pl.ds(j * local_y + row, elements, stride=REACH * local_y), :] = result[
                    j * elements : (j + 1) * elements, lane * LANES : (lane + 1) * LANES
                ]
    for lane in range(depth // LANES):
        out_ref[:, lane * LANES : (lane + 1) * LANES] = turned[lane]


def finish(place, taps, moments, before, after, parts, sizes, groups, squares):
    local_y, depth, elements = sizes[:3]
    vmem = pl.BlockSpec(memory_space=pltpu.VMEM)
    return pl.pallas_call(
        functools.partial(finish_kernel, sizes, groups, squares),
        out_shape=jax.ShapeDtypeStruct((elements * REACH * local_y, depth), jnp.float32),
        in_specs=[pl.BlockSpec(memory_space=pltpu.SMEM)] + [vmem] * (4 + len(parts)),
        out_specs=vmem,
        scratch_shapes=[
            pltpu.VMEM((depth // LANES, elements * REACH * local_y, LANES), jnp.float32)
        ],
        compiler_params=pltpu.CompilerParams(vmem_limit_bytes=VMEM_LIMIT),
        cost_estimate=pl.CostEstimate(
            flops=30 * elements * REACH * local_y * depth,
            bytes_accessed=4 * 1024 * 1024,
            transcendentals=0,
        ),
        name="finish",
    )(place, taps, moments, before, after, *parts)


def shift(values, axis, by):
    count = lax.axis_size(axis)
    return lax.ppermute(
        values, axis, [(i, i + by) for i in range(count) if 0 <= i + by < count]
    )


def turn(values, axis, by):
    count = lax.axis_size(axis)
    return lax.ppermute(values, axis, [(i, (i + by) % count) for i in range(count)])


def squared_norms(size_x, size_y, size_z):
    def of(extent):
        return sum(((2.0 * i + 1.0) / extent - 1.0) ** 2 for i in range(extent))

    return (
        float(size_x * size_y * size_z),
        of(size_x) * size_y * size_z,
        of(size_y) * size_x * size_z,
        of(size_z) * size_x * size_y,
    )


def shards(counts, kernel_taps, peak_bins, peak_share):
    local_bins, local_x, local_y, depth = counts.shape
    elements = peak_bins.shape[0]
    split = lax.axis_size("mz")
    size_x = local_x * lax.axis_size("gx")
    size_y = local_y * lax.axis_size("gy")
    devices = split * lax.axis_size("gx") * lax.axis_size("gy")
    at_m = lax.axis_index("mz")
    place = jnp.stack([lax.axis_index("gx"), lax.axis_index("gy"), at_m]).astype(jnp.int32)
    sizes = (local_bins, local_x, local_y, depth, elements, split, local_bins * split,
             size_x, size_y, devices)
    *mixed, moments = mix(place, kernel_taps, peak_bins, peak_share, counts, sizes, GROUPS)
    gathered = lax.all_to_all(moments, ("gx", "gy", "mz"), 0, 0, tiled=True)
    parts = []
    complete = {}
    for group, halves in enumerate(GROUPS):
        main, up, down = mixed[3 * group : 3 * group + 3]
        length = len(halves[0])
        from_above = shift(up, "gx", -1)
        from_below = shift(down, "gx", 1)
        spans = (slice(0, length), slice(length, 2 * length))

        def full(ahead, span):
            owner = (at_m + ahead) % split
            return (
                main[ahead, span]
                + jnp.where(owner == split - 1, from_above[span], 0.0)
                + jnp.where(owner == 0, from_below[span], 0.0)
            )

        leaf_up = turn(full(2, spans[0]), "mz", 1)
        leaf_down = turn(full(2, spans[1]), "mz", -1)
        direct_up = turn(full(1, spans[1]), "mz", 1)
        direct_down = turn(full(3, spans[0]), "mz", -1)
        late_up = turn(full(1, spans[0]) + leaf_up, "mz", 1)
        late_down = turn(full(3, spans[1]) + leaf_down, "mz", -1)
        own = full(0, slice(0, 2 * length))
        parts += [own, direct_down, direct_up, late_up, late_down]
        for half, (near, far) in enumerate(((direct_down, late_up), (direct_up, late_down))):
            for slot, row in enumerate(halves[half]):
                complete[row] = (own, half * length + slot, near, far, slot)

    def rows_of(rows):
        out = []
        for row in rows:
            own, index, near, far, slot = complete[row]
            out.append(own[index] + near[slot] + far[slot])
        return jnp.stack(out)

    before = shift(rows_of(range(local_y - REACH, local_y)), "gy", 1)
    after = shift(rows_of(range(REACH)), "gy", -1)
    result = finish(
        place, kernel_taps, gathered, before, after, parts,
        (local_y, depth, elements, split, local_x, size_x, size_y), GROUPS,
        squared_norms(size_x, size_y, depth),
    )
    return result.reshape(elements, local_x // split, local_y, depth)


def solution(mesh):
    return jax.shard_map(
        shards,
        mesh=mesh,
        in_specs=(P("mz", "gx", "gy", None), P(), P(), P()),
        out_specs=P(None, ("gx", "mz"), "gy", None),
        check_vma=False,
    )
```

```python
import functools

import jax
import jax.numpy as jnp
from jax import lax
from jax.experimental import pallas as pl
from jax.experimental.pallas import tpu as pltpu
from jax.sharding import PartitionSpec as P

RIDGE_WEIGHT = 0.5
TAPS = 5
REACH = 2
LANES = 128
HIGHEST = lax.Precision.HIGHEST
MIB = 1024 * 1024

def iota(shape, dim):
    return lax.broadcasted_iota(jnp.int32, shape, dim)


def normalized(taps_ref):
    taps = taps_ref[...]
    return taps / jnp.sum(taps, axis=1, keepdims=True)


def tap(weights, axis, offset):
    return weights[axis : axis + 1, offset : offset + 1]


def adjoint(weights, axis, positions, extent):
    ones = jnp.zeros(positions.shape, jnp.float32)
    linear = jnp.zeros(positions.shape, jnp.float32)
    for offset in range(TAPS):
        target = positions - (offset - REACH)
        inside = (target >= 0) & (target < extent)
        weight = jnp.where(inside, tap(weights, axis, offset), 0.0)
        coordinate = (2.0 * target.astype(jnp.float32) + 1.0) / float(extent) - 1.0
        ones = ones + weight
        linear = linear + weight * coordinate
    return ones, linear


def unmix_rows(bins_ref, share_ref, all_bins):
    peaks, elements = bins_ref.shape
    bins = bins_ref[...]
    share = share_ref[...]
    rows = iota((all_bins, elements), 0)
    mixing = jnp.zeros((all_bins, elements), jnp.float32)
    for peak in range(peaks):
        mixing = mixing + jnp.where(
            rows == bins[peak : peak + 1, :], share[peak : peak + 1, :], 0.0
        )

    def transposed_product(values):
        return lax.dot_general(
            mixing, values, (((0,), (0,)), ((), ())), precision=HIGHEST,
            preferred_element_type=jnp.float32,
        )

    left = transposed_product(mixing)
    full = (all_bins, all_bins)
    mixing_t = transposed_product(jnp.where(iota(full, 0) == iota(full, 1), 1.0, 0.0))
    square = (elements, elements)
    left = left + jnp.where(iota(square, 0) == iota(square, 1), RIDGE_WEIGHT, 0.0)
    right = mixing_t
    for step in range(elements):
        inverse = 1.0 / left[step : step + 1, step : step + 1]
        left_row = left[step : step + 1, :] * inverse
        right_row = right[step : step + 1, :] * inverse
        column = left[:, step : step + 1]
        here = iota((elements, 1), 0) == step
        left = jnp.where(here, left_row, left - column * left_row)
        right = jnp.where(here, right_row, right - column * right_row)
    return right


def position(axis):
    return lax.axis_index(axis)


def coordinate(at, extent):
    return (2.0 * lax.convert_element_type(at, jnp.float32) + 1.0) / float(extent) - 1.0


def split_pieces(wide):
    high = wide.astype(jnp.bfloat16)
    return high, (wide - high.astype(jnp.float32)).astype(jnp.bfloat16)


def lane_parts(depth):
    return range(depth // LANES)


def plane_of(held, row, count, stride):
    parts = [held[lane, pl.ds(row, count, stride=stride), :] for lane in range(held.shape[0])]
    return jnp.concatenate(parts, axis=1).astype(jnp.float32).astype(jnp.bfloat16)


def fill_table(table, spread, layer, targets, weights):
    elements = spread.shape[0]
    for place, target in enumerate(targets):
        factor = jnp.zeros(layer.shape, jnp.float32)
        for offset in range(TAPS):
            factor = jnp.where(layer - target + REACH == offset, tap(weights, 0, offset), factor)
        table[pl.ds(place * elements, elements), :] = spread * factor
    return split_pieces(table[...])


def product(high, low, plane):
    return jnp.dot(high, plane, preferred_element_type=jnp.float32) + jnp.dot(
        low, plane, preferred_element_type=jnp.float32
    )


def add_sums(sums, mixed, ones_y, linear_y, row, first):
    plain = mixed * ones_y[row : row + 1, :]
    tilted = mixed * linear_y[row : row + 1, :]
    if first:
        sums[0], sums[1] = plain, tilted
    else:
        sums[0] += plain
        sums[1] += tilted


def plane_moments(parts, sums, targets, elements, local_x, size_x):
    for place, target in enumerate(targets):
        x = position("gx") * local_x + target
        inside = jnp.where((x >= 0) & (x < size_x), 1.0, 0.0)
        rows = pl.ds(place * elements, elements)
        plain = sums[0, rows, :] * inside
        parts[0] = parts[0] + plain
        parts[1] = parts[1] + plain * coordinate(x, size_x)
        parts[2] = parts[2] + sums[1, rows, :] * inside
    return parts


def mix_kernel(sizes, taps_hbm, bins_hbm, share_hbm, counts_ref, main_ref, up_ref, down_ref, moments_ref,
               taps_ref, bins_ref, share_ref, held, table, sums, small_sem, sem):
    local_bins, local_x, local_y, depth, elements, split, all_bins, size_x, size_y = sizes
    rows_in = local_bins * local_x
    small = [
        pltpu.make_async_copy(source, target, small_sem.at[i])
        for i, (source, target) in enumerate(
            ((taps_hbm, taps_ref), (bins_hbm, bins_ref), (share_hbm, share_ref))
        )
    ]
    copies = [
        pltpu.make_async_copy(
            counts_ref.at[:, pl.ds(lane * LANES, LANES)], held.at[lane], sem.at[lane]
        )
        for lane in lane_parts(depth)
    ]
    for copy in small + copies:
        copy.start()
    for copy in small:
        copy.wait()
    weights = normalized(taps_ref)
    unmix = unmix_rows(bins_ref, share_ref, all_bins)
    shape = (all_bins, rows_in)
    expand = jnp.where(
        iota(shape, 0) == position("mz") * local_bins + iota(shape, 1) // local_x, 1.0, 0.0
    )
    spread = jnp.dot(unmix, expand, precision=HIGHEST, preferred_element_type=jnp.float32)
    layer = iota((1, rows_in), 1) % local_x
    targets = []
    for ahead in range(split):
        owner = (position("mz") + ahead) % split
        targets += [owner * REACH + j for j in range(REACH)]
    targets += [j - REACH for j in range(REACH)] + [local_x + j for j in range(REACH)]
    high, low = fill_table(table, spread, layer, targets, weights)
    rows_y = position("gy") * local_y + iota((local_y, depth), 0)
    ones_y, linear_y = adjoint(weights, 1, rows_y, size_y)
    block = REACH * elements
    for copy in copies:
        copy.wait()
    for row in range(local_y):
        mixed = product(high, low, plane_of(held, row, rows_in, local_y))
        for ahead in range(split):
            main_ref[ahead, row] = mixed[ahead * block : (ahead + 1) * block]
        up_ref[row] = mixed[split * block : (split + 1) * block]
        down_ref[row] = mixed[(split + 1) * block :]
        add_sums(sums, mixed, ones_y, linear_y, row, row == 0)
    parts = [jnp.zeros((elements, depth), jnp.float32) for _ in range(3)]
    parts = plane_moments(parts, sums, targets, elements, local_x, size_x)
    rest = jnp.zeros((LANES - 4 * elements, depth), jnp.float32)
    stacked = jnp.concatenate([parts[0], parts[1], parts[2], parts[0], rest], axis=0)
    ones_z, linear_z = adjoint(weights, 2, iota((8, depth), 1), depth)
    profile = jnp.where(iota((8, depth), 0) == 0, ones_z, linear_z)
    products = lax.dot_general(
        profile, stacked, (((1,), (1,)), ((), ())), precision=HIGHEST,
        preferred_element_type=jnp.float32,
    )
    row = jnp.where(iota((1, LANES), 1) < 3 * elements, products[0:1], products[1:2])
    moments_ref[...] = jnp.broadcast_to(row, moments_ref.shape)


def mix(taps, bins, share, counts, sizes, peers):
    local_bins, local_x, local_y, depth, elements, split, _, _, _ = sizes
    block = REACH * elements
    rows_in = local_bins * local_x
    rows_out = (split + 2) * block
    vmem = pl.BlockSpec(memory_space=pltpu.VMEM)
    hbm = pl.BlockSpec(memory_space=pltpu.HBM)
    shapes = [(split, local_y, block, depth)] + [(local_y, block, depth)] * 2 + [(8, LANES)]
    return pl.pallas_call(
        functools.partial(mix_kernel, sizes),
        out_shape=[jax.ShapeDtypeStruct(shape, jnp.float32) for shape in shapes],
        in_specs=[hbm] * 4,
        out_specs=[vmem] * len(shapes),
        scratch_shapes=[
            pltpu.VMEM(taps.shape, jnp.float32),
            pltpu.VMEM(bins.shape, jnp.int32),
            pltpu.VMEM(share.shape, jnp.float32),
            pltpu.VMEM((depth // LANES, rows_in * local_y, LANES), jnp.int32),
            pltpu.VMEM((rows_out, rows_in), jnp.float32),
            pltpu.VMEM((2, rows_out, depth), jnp.float32),
            pltpu.SemaphoreType.DMA((3,)),
            pltpu.SemaphoreType.DMA((depth // LANES,)),
        ],
        compiler_params=pltpu.CompilerParams(vmem_limit_bytes=12 * MIB),
        cost_estimate=pl.CostEstimate(
            flops=4 * rows_out * rows_in * local_y * depth,
            bytes_accessed=8 << 20,
            transcendentals=0,
        ),
        name="mix_bins",
    )(*[
        pltpu.with_memory_space_constraint(values, pltpu.HBM)
        for values in (taps, bins, share, counts.reshape(-1, depth))
    ])


def owner_flags(ahead, split):
    owner = (position("mz") + ahead) % split
    above = jnp.where(owner == split - 1, 1.0, 0.0)
    below = jnp.where(owner == 0, 1.0, 0.0)
    return above, below


def with_edges(main_ref, above_ref, below_ref, flags, ahead, row):
    return main_ref[ahead, row] + flags[0] * above_ref[row] + flags[1] * below_ref[row]


def rows_at(slot, block):
    return pl.ds(slot * block, block)


def add_kernel(*refs):
    total = refs[0][...]
    for ref in refs[1:-1]:
        total = total + ref[...]
    refs[-1][...] = total


def peers_kernel(gathered_ref, out_ref):
    total = gathered_ref[0:8]
    for peer in range(1, gathered_ref.shape[0] // 8):
        total = total + gathered_ref[8 * peer : 8 * peer + 8]
    out_ref[...] = total


def first_kernel(split, half, main_ref, above_ref, below_ref, moments_ref, other_ref, up_ref, down_ref,
                 spread_ref):
    block = main_ref.shape[2]
    total = moments_ref[...] + other_ref[...]
    for peer in range(spread_ref.shape[0] // 8):
        spread_ref[8 * peer : 8 * peer + 8] = total
    for out, pieces in ((up_ref, ((2, 0), (1, half))), (down_ref, ((2, half), (3, 0)))):
        for place, (ahead, base) in enumerate(pieces):
            flags = owner_flags(ahead, split)
            for slot in range(half):
                out[rows_at(place * half + slot, block), :] = with_edges(
                    main_ref, above_ref, below_ref, flags, ahead, base + slot
                )


def late_kernel(split, half, main_ref, above_ref, below_ref, up_ref, down_ref, gathered_ref,
                late_up, late_down, summed_ref):
    peers_kernel(gathered_ref, summed_ref)
    block = main_ref.shape[2]
    for ahead, base, leaf, out in ((1, 0, up_ref, late_up), (3, half, down_ref, late_down)):
        flags = owner_flags(ahead, split)
        for slot in range(half):
            rows = rows_at(slot, block)
            value = with_edges(main_ref, above_ref, below_ref, flags, ahead, base + slot)
            out[rows, :] = value + leaf[rows, :]


def own_kernel(split, half, main_ref, above_ref, below_ref, up_ref, down_ref, out_ref):
    block = main_ref.shape[2]
    flags = owner_flags(0, split)
    for row in range(2 * half):
        direct = down_ref if row < half else up_ref
        out_ref[rows_at(row, block), :] = (
            with_edges(main_ref, above_ref, below_ref, flags, 0, row)
            + direct[rows_at(half + row % half, block), :]
        )


def rim_kernel(half, block, own_ref, late_up, late_down, moments_ref, other_ref,
               low_ref, high_ref, summed_ref):
    summed_ref[...] = moments_ref[...] + other_ref[...]
    low, high = pl.ds(0, REACH * block), pl.ds((half - REACH) * block, REACH * block)
    low_ref[...] = own_ref[low, :] + late_up[low, :]
    high_ref[...] = own_ref[pl.ds((2 * half - REACH) * block, REACH * block), :] + late_down[high, :]


def local_call(kernel, shapes, args, name, weight=1):
    vmem = pl.BlockSpec(memory_space=pltpu.VMEM)
    size = sum(a.size for a in args) * 4 * weight
    return pl.pallas_call(
        kernel,
        out_shape=[jax.ShapeDtypeStruct(shape, jnp.float32) for shape in shapes],
        in_specs=[vmem] * len(args),
        out_specs=[vmem] * len(shapes),
        compiler_params=pltpu.CompilerParams(vmem_limit_bytes=4 * MIB),
        cost_estimate=pl.CostEstimate(flops=size, bytes_accessed=size, transcendentals=0),
        name=name,
    )(*args)


def finish_kernel(sizes, squares, taps_hbm, before_ref, after_ref, low_ref, high_ref,
                  own_ref, late_up, late_down, *rest):
    moments, (out_ref, taps_ref, turned, sem) = rest[:-4], rest[-4:]
    local_y, depth, elements, split, local_x, size_x, size_y = sizes
    copy = pltpu.make_async_copy(taps_hbm, taps_ref, sem)
    copy.start()
    half = local_y // 2
    block = REACH * elements
    copy.wait()
    weights = normalized(taps_ref)
    planes = {}
    for j in range(REACH):
        rows = rows_at(j, block)
        planes[j - REACH] = before_ref[rows, :]
        planes[local_y + j] = after_ref[rows, :]
        planes[j] = low_ref[rows, :]
        planes[local_y - REACH + j] = high_ref[rows, :]
    for row in range(REACH, local_y - REACH):
        late = late_up if row < half else late_down
        planes[row] = own_ref[rows_at(row, block), :] + late[rows_at(row % half, block), :]
    totals = moments[0][0:1]
    for other in moments[1:]:
        totals = totals + other[0:1]
    lanes = iota((elements, LANES), 1)
    rows = iota((elements, LANES), 0)
    fitted = [
        jnp.sum(jnp.where(lanes == rows + j * elements, totals, 0.0), axis=1, keepdims=True)
        / squares[j]
        for j in range(4)
    ]
    at = position("gx") * local_x + position("mz") * REACH
    base = jnp.concatenate(
        [fitted[0] + fitted[1] * coordinate(at + j, size_x) for j in range(REACH)], axis=0
    )
    slope_y = jnp.concatenate([fitted[2]] * REACH, axis=0)
    slope_z = jnp.concatenate([fitted[3]] * REACH, axis=0)
    line = iota((1, depth), 1)
    tilted = base + slope_z * coordinate(line, depth)
    edge = []
    for offset in range(TAPS):
        source = line + (offset - REACH)
        edge.append(jnp.where((source >= 0) & (source < depth), tap(weights, 2, offset), 0.0))
    for row in range(local_y):
        smooth = tap(weights, 1, 0) * planes[row - REACH]
        for offset in range(1, TAPS):
            smooth = smooth + tap(weights, 1, offset) * planes[row + offset - REACH]
        result = -(tilted + slope_y * coordinate(position("gy") * local_y + row, size_y))
        for offset in range(TAPS):
            shifted = smooth if offset == REACH else pltpu.roll(smooth, (REACH - offset) % depth, 1)
            result = result + edge[offset] * shifted
        for j in range(REACH):
            for lane in lane_parts(depth):
                turned[lane, pl.ds(j * local_y + row, elements, stride=REACH * local_y), :] = result[
                    j * elements : (j + 1) * elements, lane * LANES : (lane + 1) * LANES
                ]
    for lane in lane_parts(depth):
        out_ref[:, lane * LANES : (lane + 1) * LANES] = turned[lane]


def finish(taps, args, sizes, squares):
    local_y, depth, elements = sizes[:3]
    vmem = pl.BlockSpec(memory_space=pltpu.VMEM)
    hbm = pl.BlockSpec(memory_space=pltpu.HBM)
    rows = elements * REACH * local_y
    return pl.pallas_call(
        functools.partial(finish_kernel, sizes, squares),
        out_shape=jax.ShapeDtypeStruct((rows, depth), jnp.float32),
        in_specs=[hbm] + [vmem] * len(args),
        out_specs=vmem,
        scratch_shapes=[
            pltpu.VMEM(taps.shape, jnp.float32),
            pltpu.VMEM((depth // LANES, rows, LANES), jnp.float32),
            pltpu.SemaphoreType.DMA,
        ],
        compiler_params=pltpu.CompilerParams(vmem_limit_bytes=8 * MIB),
        cost_estimate=pl.CostEstimate(
            flops=30 * rows * depth, bytes_accessed=4 << 20, transcendentals=0
        ),
        name="finish",
    )(pltpu.with_memory_space_constraint(taps, pltpu.HBM), *args)


def shift(values, axis, by):
    count = lax.axis_size(axis)
    return lax.ppermute(
        values, axis, [(i, i + by) for i in range(count) if 0 <= i + by < count]
    )


def turn(values, axis, by):
    count = lax.axis_size(axis)
    return lax.ppermute(values, axis, [(i, (i + by) % count) for i in range(count)])


def squared_norms(size_x, size_y, size_z):
    def of(extent):
        return sum(((2.0 * i + 1.0) / extent - 1.0) ** 2 for i in range(extent))

    return (
        float(size_x * size_y * size_z),
        of(size_x) * size_y * size_z,
        of(size_y) * size_x * size_z,
        of(size_z) * size_x * size_y,
    )


def shards(counts, kernel_taps, peak_bins, peak_share):
    local_bins, local_x, local_y, depth = counts.shape
    elements = peak_bins.shape[0]
    split = lax.axis_size("mz")
    across = lax.axis_size("gx")
    along = lax.axis_size("gy")
    size_x = local_x * across
    size_y = local_y * along
    half = local_y // 2
    block = REACH * elements
    sizes = (local_bins, local_x, local_y, depth, elements, split, local_bins * split, size_x, size_y)
    tile = (8, LANES)
    main, up, down, moments = mix(
        kernel_taps, peak_bins.T, peak_share.T, counts, sizes, across * split
    )
    from_above = shift(up, "gx", -1)
    from_below = shift(down, "gx", 1)
    (moments,) = local_call(add_kernel, [tile], (moments, turn(moments, "mz", 1)), "add_sums")
    blocks = (main, from_above, from_below)
    both = (2 * half * block, depth)
    whole = (half * block, depth)
    up, down, spread = local_call(
        functools.partial(first_kernel, split, half), [both, both, (8 * along, LANES)],
        blocks + (moments, turn(moments, "mz", 2)), "first_blocks",
    )
    up = turn(up, "mz", 1)
    down = turn(down, "mz", -1)
    gathered = lax.all_to_all(spread, "gy", 0, 0, tiled=True)
    late_up, late_down, moments = local_call(
        functools.partial(late_kernel, split, half), [whole, whole, tile],
        blocks + (up, down, gathered), "late_blocks",
    )
    late_up = turn(late_up, "mz", 1)
    late_down = turn(late_down, "mz", -1)
    (own,) = local_call(
        functools.partial(own_kernel, split, half), [(local_y * block, depth)],
        blocks + (up, down), "own_blocks",
    )
    (moments,) = local_call(add_kernel, [tile], (moments, turn(moments, "gx", 1)), "add_sums")
    rim = (REACH * block, depth)
    low, high, moments = local_call(
        functools.partial(rim_kernel, half, block), [rim, rim, tile],
        (own, late_up, late_down, moments, turn(moments, "gx", 2)), "rim_blocks",
    )
    before = shift(high, "gy", 1)
    after = shift(low, "gy", -1)
    result = finish(
        kernel_taps,
        (before, after, low, high, own, late_up, late_down, moments),
        (local_y, depth, elements, split, local_x, size_x, size_y),
        squared_norms(size_x, size_y, depth),
    )
    return result.reshape(elements, local_x // split, local_y, depth)


def solution(mesh):
    return jax.shard_map(
        shards,
        mesh=mesh,
        in_specs=(P("mz", "gx", "gy", None), P(), P(), P()),
        out_specs=P(None, ("gx", "mz"), "gy", None),
        check_vma=False,
    )
```

```python
import functools

import jax
import jax.numpy as jnp
from jax import lax
from jax.experimental import pallas as pl
from jax.experimental.pallas import tpu as pltpu
from jax.sharding import PartitionSpec as P

RIDGE_WEIGHT = 0.5
TAPS = 5
REACH = 2
LANES = 128
HIGHEST = lax.Precision.HIGHEST
MIB = 1024 * 1024

def iota(shape, dim):
    return lax.broadcasted_iota(jnp.int32, shape, dim)


def normalized(taps_ref):
    taps = taps_ref[...]
    return taps / jnp.sum(taps, axis=1, keepdims=True)


def tap(weights, axis, offset):
    return weights[axis : axis + 1, offset : offset + 1]


def adjoint(weights, axis, positions, extent):
    ones = jnp.zeros(positions.shape, jnp.float32)
    linear = jnp.zeros(positions.shape, jnp.float32)
    for offset in range(TAPS):
        target = positions - (offset - REACH)
        inside = (target >= 0) & (target < extent)
        weight = jnp.where(inside, tap(weights, axis, offset), 0.0)
        coordinate = (2.0 * target.astype(jnp.float32) + 1.0) / float(extent) - 1.0
        ones = ones + weight
        linear = linear + weight * coordinate
    return ones, linear


def unmix_rows(bins_ref, share_ref, all_bins):
    peaks, elements = bins_ref.shape
    bins = bins_ref[...]
    share = share_ref[...]
    rows = iota((all_bins, elements), 0)
    mixing = jnp.zeros((all_bins, elements), jnp.float32)
    for peak in range(peaks):
        mixing = mixing + jnp.where(
            rows == bins[peak : peak + 1, :], share[peak : peak + 1, :], 0.0
        )

    def transposed_product(values):
        return lax.dot_general(
            mixing, values, (((0,), (0,)), ((), ())), precision=HIGHEST,
            preferred_element_type=jnp.float32,
        )

    left = transposed_product(mixing)
    full = (all_bins, all_bins)
    mixing_t = transposed_product(jnp.where(iota(full, 0) == iota(full, 1), 1.0, 0.0))
    square = (elements, elements)
    left = left + jnp.where(iota(square, 0) == iota(square, 1), RIDGE_WEIGHT, 0.0)
    right = mixing_t
    for step in range(elements):
        inverse = 1.0 / left[step : step + 1, step : step + 1]
        left_row = left[step : step + 1, :] * inverse
        right_row = right[step : step + 1, :] * inverse
        column = left[:, step : step + 1]
        here = iota((elements, 1), 0) == step
        left = jnp.where(here, left_row, left - column * left_row)
        right = jnp.where(here, right_row, right - column * right_row)
    return right


def position(axis):
    return lax.axis_index(axis)


def coordinate(at, extent):
    return (2.0 * lax.convert_element_type(at, jnp.float32) + 1.0) / float(extent) - 1.0


def split_pieces(wide):
    high = wide.astype(jnp.bfloat16)
    return high, (wide - high.astype(jnp.float32)).astype(jnp.bfloat16)


def lane_parts(depth):
    return range(depth // LANES)


def plane_of(held, row, count, stride):
    parts = [held[lane, pl.ds(row, count, stride=stride), :] for lane in range(held.shape[0])]
    return jnp.concatenate(parts, axis=1).astype(jnp.float32).astype(jnp.bfloat16)


def fill_table(table, spread, layer, targets, weights):
    elements = spread.shape[0]
    for place, target in enumerate(targets):
        factor = jnp.zeros(layer.shape, jnp.float32)
        for offset in range(TAPS):
            factor = jnp.where(layer - target + REACH == offset, tap(weights, 0, offset), factor)
        table[pl.ds(place * elements, elements), :] = spread * factor
    return split_pieces(table[...])


def product(high, low, plane):
    return jnp.dot(high, plane, preferred_element_type=jnp.float32) + jnp.dot(
        low, plane, preferred_element_type=jnp.float32
    )


def add_sums(sums, mixed, ones_y, linear_y, row, first):
    plain = mixed * ones_y[row : row + 1, :]
    tilted = mixed * linear_y[row : row + 1, :]
    if first:
        sums[0], sums[1] = plain, tilted
    else:
        sums[0] += plain
        sums[1] += tilted


def plane_moments(parts, sums, targets, elements, local_x, size_x):
    for place, target in enumerate(targets):
        x = position("gx") * local_x + target
        inside = jnp.where((x >= 0) & (x < size_x), 1.0, 0.0)
        rows = pl.ds(place * elements, elements)
        plain = sums[0, rows, :] * inside
        parts[0] = parts[0] + plain
        parts[1] = parts[1] + plain * coordinate(x, size_x)
        parts[2] = parts[2] + sums[1, rows, :] * inside
    return parts


def mix_kernel(sizes, taps_hbm, bins_hbm, share_hbm, counts_ref, main_ref, up_ref, down_ref, moments_ref,
               taps_ref, bins_ref, share_ref, held, table, sums, small_sem, sem):
    local_bins, local_x, local_y, depth, elements, split, all_bins, size_x, size_y = sizes
    rows_in = local_bins * local_x
    small = [
        pltpu.make_async_copy(source, target, small_sem.at[i])
        for i, (source, target) in enumerate(
            ((taps_hbm, taps_ref), (bins_hbm, bins_ref), (share_hbm, share_ref))
        )
    ]
    copies = [
        pltpu.make_async_copy(
            counts_ref.at[:, pl.ds(lane * LANES, LANES)], held.at[lane], sem.at[lane]
        )
        for lane in lane_parts(depth)
    ]
    for copy in small + copies:
        copy.start()
    for copy in small:
        copy.wait()
    weights = normalized(taps_ref)
    unmix = unmix_rows(bins_ref, share_ref, all_bins)
    shape = (all_bins, rows_in)
    expand = jnp.where(
        iota(shape, 0) == position("mz") * local_bins + iota(shape, 1) // local_x, 1.0, 0.0
    )
    spread = jnp.dot(unmix, expand, precision=HIGHEST, preferred_element_type=jnp.float32)
    layer = iota((1, rows_in), 1) % local_x
    targets = []
    for ahead in range(split):
        owner = (position("mz") + ahead) % split
        targets += [owner * REACH + j for j in range(REACH)]
    targets += [j - REACH for j in range(REACH)] + [local_x + j for j in range(REACH)]
    high, low = fill_table(table, spread, layer, targets, weights)
    rows_y = position("gy") * local_y + iota((local_y, depth), 0)
    ones_y, linear_y = adjoint(weights, 1, rows_y, size_y)
    block = REACH * elements
    for copy in copies:
        copy.wait()
    for row in range(local_y):
        mixed = product(high, low, plane_of(held, row, rows_in, local_y))
        for ahead in range(split):
            main_ref[ahead, row] = mixed[ahead * block : (ahead + 1) * block]
        up_ref[row] = mixed[split * block : (split + 1) * block]
        down_ref[row] = mixed[(split + 1) * block :]
        add_sums(sums, mixed, ones_y, linear_y, row, row == 0)
    parts = [jnp.zeros((elements, depth), jnp.float32) for _ in range(3)]
    parts = plane_moments(parts, sums, targets, elements, local_x, size_x)
    rest = jnp.zeros((LANES - 4 * elements, depth), jnp.float32)
    stacked = jnp.concatenate([parts[0], parts[1], parts[2], parts[0], rest], axis=0)
    ones_z, linear_z = adjoint(weights, 2, iota((8, depth), 1), depth)
    profile = jnp.where(iota((8, depth), 0) == 0, ones_z, linear_z)
    products = lax.dot_general(
        profile, stacked, (((1,), (1,)), ((), ())), precision=HIGHEST,
        preferred_element_type=jnp.float32,
    )
    row = jnp.where(iota((1, LANES), 1) < 3 * elements, products[0:1], products[1:2])
    moments_ref[...] = jnp.broadcast_to(row, moments_ref.shape)


def mix(taps, bins, share, counts, sizes, peers):
    local_bins, local_x, local_y, depth, elements, split, _, _, _ = sizes
    block = REACH * elements
    rows_in = local_bins * local_x
    rows_out = (split + 2) * block
    vmem = pl.BlockSpec(memory_space=pltpu.VMEM)
    hbm = pl.BlockSpec(memory_space=pltpu.HBM)
    shapes = [(split, local_y, block, depth)] + [(local_y, block, depth)] * 2 + [(8, LANES)]
    return pl.pallas_call(
        functools.partial(mix_kernel, sizes),
        out_shape=[jax.ShapeDtypeStruct(shape, jnp.float32) for shape in shapes],
        in_specs=[hbm] * 4,
        out_specs=[vmem] * len(shapes),
        scratch_shapes=[
            pltpu.VMEM(taps.shape, jnp.float32),
            pltpu.VMEM(bins.shape, jnp.int32),
            pltpu.VMEM(share.shape, jnp.float32),
            pltpu.VMEM((depth // LANES, rows_in * local_y, LANES), jnp.int32),
            pltpu.VMEM((rows_out, rows_in), jnp.float32),
            pltpu.VMEM((2, rows_out, depth), jnp.float32),
            pltpu.SemaphoreType.DMA((3,)),
            pltpu.SemaphoreType.DMA((depth // LANES,)),
        ],
        compiler_params=pltpu.CompilerParams(vmem_limit_bytes=12 * MIB),
        cost_estimate=pl.CostEstimate(
            flops=4 * rows_out * rows_in * local_y * depth,
            bytes_accessed=8 << 20,
            transcendentals=0,
        ),
        name="mix_bins",
    )(*[
        pltpu.with_memory_space_constraint(values, pltpu.HBM)
        for values in (taps, bins, share, counts.reshape(-1, depth))
    ])


def owner_flags(ahead, split):
    owner = (position("mz") + ahead) % split
    above = jnp.where(owner == split - 1, 1.0, 0.0)
    below = jnp.where(owner == 0, 1.0, 0.0)
    return above, below


def with_edges(main_ref, above_ref, below_ref, flags, ahead, row):
    return main_ref[ahead, row] + flags[0] * above_ref[row] + flags[1] * below_ref[row]


def rows_at(slot, block):
    return pl.ds(slot * block, block)


def add_kernel(*refs):
    total = refs[0][...]
    for ref in refs[1:-1]:
        total = total + ref[...]
    refs[-1][...] = total


def first_kernel(split, half, main_ref, above_ref, below_ref, moments_ref, other_ref, up_ref, down_ref,
                 spread_ref):
    block = main_ref.shape[2]
    total = moments_ref[...] + other_ref[...]
    spread_ref[...] = jnp.broadcast_to(total[0:1], spread_ref.shape)
    for out, pieces in ((up_ref, ((2, 0), (1, half))), (down_ref, ((2, half), (3, 0)))):
        for place, (ahead, base) in enumerate(pieces):
            flags = owner_flags(ahead, split)
            for slot in range(half):
                out[rows_at(place * half + slot, block), :] = with_edges(
                    main_ref, above_ref, below_ref, flags, ahead, base + slot
                )


def late_kernel(split, half, main_ref, above_ref, below_ref, up_ref, down_ref, gathered_ref,
                early_up, early_down, late_up, late_down, summed_ref):
    total = jnp.sum(gathered_ref[...], axis=0, keepdims=True)
    summed_ref[...] = jnp.broadcast_to(total, summed_ref.shape)
    block = main_ref.shape[2]
    for ahead, base, leaf, early, late, rim in (
        (1, 0, up_ref, early_up, late_up, 0), (3, half, down_ref, early_down, late_down, half - REACH)
    ):
        flags = owner_flags(ahead, split)
        for slot in range(half):
            value = with_edges(main_ref, above_ref, below_ref, flags, ahead, base + slot)
            value = value + leaf[rows_at(slot, block), :]
            if rim <= slot < rim + REACH:
                early[rows_at(slot - rim, block), :] = value
            else:
                late[rows_at(slot if rim else slot - REACH, block), :] = value


def own_kernel(split, half, main_ref, above_ref, below_ref, up_ref, down_ref, out_ref):
    block = main_ref.shape[2]
    flags = owner_flags(0, split)
    for row in range(2 * half):
        direct = down_ref if row < half else up_ref
        out_ref[rows_at(row, block), :] = (
            with_edges(main_ref, above_ref, below_ref, flags, 0, row)
            + direct[rows_at(half + row % half, block), :]
        )


def rim_kernel(half, block, own_ref, early_up, early_down, low_ref, high_ref):
    rim = REACH * block
    low_ref[...] = own_ref[pl.ds(0, rim), :] + early_up[...]
    high_ref[...] = own_ref[pl.ds(2 * half * block - rim, rim), :] + early_down[...]


def local_call(kernel, shapes, args, name, weight=1):
    vmem = pl.BlockSpec(memory_space=pltpu.VMEM)
    size = sum(a.size for a in args) * 4 * weight
    return pl.pallas_call(
        kernel,
        out_shape=[jax.ShapeDtypeStruct(shape, jnp.float32) for shape in shapes],
        in_specs=[vmem] * len(args),
        out_specs=[vmem] * len(shapes),
        compiler_params=pltpu.CompilerParams(vmem_limit_bytes=4 * MIB),
        cost_estimate=pl.CostEstimate(flops=size, bytes_accessed=size, transcendentals=0),
        name=name,
    )(*args)


def finish_kernel(sizes, squares, taps_hbm, before_ref, after_ref, low_ref, high_ref,
                  own_ref, late_up, late_down, *rest):
    moments, (out_ref, taps_ref, turned, sem) = rest[:-4], rest[-4:]
    local_y, depth, elements, split, local_x, size_x, size_y = sizes
    copy = pltpu.make_async_copy(taps_hbm, taps_ref, sem)
    copy.start()
    half = local_y // 2
    block = REACH * elements
    copy.wait()
    weights = normalized(taps_ref)
    planes = {}
    for j in range(REACH):
        rows = rows_at(j, block)
        planes[j - REACH] = before_ref[rows, :]
        planes[local_y + j] = after_ref[rows, :]
        planes[j] = low_ref[rows, :]
        planes[local_y - REACH + j] = high_ref[rows, :]
    for row in range(REACH, local_y - REACH):
        late, slot = (late_up, row - REACH) if row < half else (late_down, row - half)
        planes[row] = own_ref[rows_at(row, block), :] + late[rows_at(slot, block), :]
    totals = moments[0][0:1]
    for other in moments[1:]:
        totals = totals + other[0:1]
    lanes = iota((elements, LANES), 1)
    rows = iota((elements, LANES), 0)
    fitted = [
        jnp.sum(jnp.where(lanes == rows + j * elements, totals, 0.0), axis=1, keepdims=True)
        / squares[j]
        for j in range(4)
    ]
    at = position("gx") * local_x + position("mz") * REACH
    base = jnp.concatenate(
        [fitted[0] + fitted[1] * coordinate(at + j, size_x) for j in range(REACH)], axis=0
    )
    slope_y = jnp.concatenate([fitted[2]] * REACH, axis=0)
    slope_z = jnp.concatenate([fitted[3]] * REACH, axis=0)
    line = iota((1, depth), 1)
    tilted = base + slope_z * coordinate(line, depth)
    edge = []
    for offset in range(TAPS):
        source = line + (offset - REACH)
        edge.append(jnp.where((source >= 0) & (source < depth), tap(weights, 2, offset), 0.0))
    for row in range(local_y):
        smooth = tap(weights, 1, 0) * planes[row - REACH]
        for offset in range(1, TAPS):
            smooth = smooth + tap(weights, 1, offset) * planes[row + offset - REACH]
        result = -(tilted + slope_y * coordinate(position("gy") * local_y + row, size_y))
        for offset in range(TAPS):
            shifted = smooth if offset == REACH else pltpu.roll(smooth, (REACH - offset) % depth, 1)
            result = result + edge[offset] * shifted
        for j in range(REACH):
            for lane in lane_parts(depth):
                turned[lane, pl.ds(j * local_y + row, elements, stride=REACH * local_y), :] = result[
                    j * elements : (j + 1) * elements, lane * LANES : (lane + 1) * LANES
                ]
    for lane in lane_parts(depth):
        out_ref[:, lane * LANES : (lane + 1) * LANES] = turned[lane]


def finish(taps, args, sizes, squares):
    local_y, depth, elements = sizes[:3]
    vmem = pl.BlockSpec(memory_space=pltpu.VMEM)
    hbm = pl.BlockSpec(memory_space=pltpu.HBM)
    rows = elements * REACH * local_y
    return pl.pallas_call(
        functools.partial(finish_kernel, sizes, squares),
        out_shape=jax.ShapeDtypeStruct((rows, depth), jnp.float32),
        in_specs=[hbm] + [vmem] * len(args),
        out_specs=vmem,
        scratch_shapes=[
            pltpu.VMEM(taps.shape, jnp.float32),
            pltpu.VMEM((depth // LANES, rows, LANES), jnp.float32),
            pltpu.SemaphoreType.DMA,
        ],
        compiler_params=pltpu.CompilerParams(vmem_limit_bytes=8 * MIB),
        cost_estimate=pl.CostEstimate(
            flops=30 * rows * depth, bytes_accessed=4 << 20, transcendentals=0
        ),
        name="finish",
    )(pltpu.with_memory_space_constraint(taps, pltpu.HBM), *args)


def shift(values, axis, by):
    count = lax.axis_size(axis)
    return lax.ppermute(
        values, axis, [(i, i + by) for i in range(count) if 0 <= i + by < count]
    )


def turn(values, axis, by):
    count = lax.axis_size(axis)
    return lax.ppermute(values, axis, [(i, (i + by) % count) for i in range(count)])


def swap(values, axis, bit):
    return lax.ppermute(values, axis, [(i, i ^ bit) for i in range(lax.axis_size(axis))])


def squared_norms(size_x, size_y, size_z):
    def of(extent):
        return sum(((2.0 * i + 1.0) / extent - 1.0) ** 2 for i in range(extent))

    return (
        float(size_x * size_y * size_z),
        of(size_x) * size_y * size_z,
        of(size_y) * size_x * size_z,
        of(size_z) * size_x * size_y,
    )


def shards(counts, kernel_taps, peak_bins, peak_share):
    local_bins, local_x, local_y, depth = counts.shape
    elements = peak_bins.shape[0]
    split = lax.axis_size("mz")
    across = lax.axis_size("gx")
    along = lax.axis_size("gy")
    size_x = local_x * across
    size_y = local_y * along
    half = local_y // 2
    block = REACH * elements
    sizes = (local_bins, local_x, local_y, depth, elements, split, local_bins * split, size_x, size_y)
    tile = (8, LANES)
    main, up, down, moments = mix(
        kernel_taps, peak_bins.T, peak_share.T, counts, sizes, across * split
    )
    from_above = shift(up, "gx", -1)
    from_below = shift(down, "gx", 1)
    for axis, by in (("gx", 1), ("mz", 1)):
        (moments,) = local_call(add_kernel, [tile], (moments, swap(moments, axis, by)), "add_sums")
    blocks = (main, from_above, from_below)
    both = (2 * half * block, depth)
    whole = (half * block, depth)
    up, down, spread = local_call(
        functools.partial(first_kernel, split, half), [both, both, (along, LANES)],
        blocks + (moments, swap(moments, "mz", 2)), "first_blocks",
    )
    up = turn(up, "mz", 1)
    down = turn(down, "mz", -1)
    gathered = lax.all_to_all(spread, "gy", 0, 0, tiled=True)
    rim = (REACH * block, depth)
    inner = ((half - REACH) * block, depth)
    early_up, early_down, late_up, late_down, moments = local_call(
        functools.partial(late_kernel, split, half), [rim, rim, inner, inner, tile],
        blocks + (up, down, gathered), "late_blocks",
    )
    early_up = turn(early_up, "mz", 1)
    early_down = turn(early_down, "mz", -1)
    late_up = turn(late_up, "mz", 1)
    late_down = turn(late_down, "mz", -1)
    (own,) = local_call(
        functools.partial(own_kernel, split, half), [(local_y * block, depth)],
        blocks + (up, down), "own_blocks",
    )
    low, high = local_call(
        functools.partial(rim_kernel, half, block), [rim, rim], (own, early_up, early_down), "rim_blocks"
    )
    before = shift(high, "gy", 1)
    after = shift(low, "gy", -1)
    result = finish(
        kernel_taps,
        (before, after, low, high, own, late_up, late_down, moments, swap(moments, "gx", 2)),
        (local_y, depth, elements, split, local_x, size_x, size_y),
        squared_norms(size_x, size_y, depth),
    )
    return result.reshape(elements, local_x // split, local_y, depth)


def solution(mesh):
    return jax.shard_map(
        shards,
        mesh=mesh,
        in_specs=(P("mz", "gx", "gy", None), P(), P(), P()),
        out_specs=P(None, ("gx", "mz"), "gy", None),
        check_vma=False,
    )
```

```python
import functools

import jax
import jax.numpy as jnp
from jax import lax
from jax.experimental import pallas as pl
from jax.experimental.pallas import tpu as pltpu
from jax.sharding import PartitionSpec as P

RIDGE_WEIGHT = 0.5
TAPS = 5
REACH = 2
LANES = 128
HIGHEST = lax.Precision.HIGHEST
MIB = 1024 * 1024

def iota(shape, dim):
    return lax.broadcasted_iota(jnp.int32, shape, dim)


def normalized(taps_ref):
    taps = taps_ref[...]
    return taps / jnp.sum(taps, axis=1, keepdims=True)


def tap(weights, axis, offset):
    return weights[axis : axis + 1, offset : offset + 1]


def adjoint(weights, axis, positions, extent):
    ones = jnp.zeros(positions.shape, jnp.float32)
    linear = jnp.zeros(positions.shape, jnp.float32)
    for offset in range(TAPS):
        target = positions - (offset - REACH)
        inside = (target >= 0) & (target < extent)
        weight = jnp.where(inside, tap(weights, axis, offset), 0.0)
        coordinate = (2.0 * target.astype(jnp.float32) + 1.0) / float(extent) - 1.0
        ones = ones + weight
        linear = linear + weight * coordinate
    return ones, linear


def unmix_rows(bins_ref, share_ref, all_bins):
    peaks, elements = bins_ref.shape
    bins = bins_ref[...]
    share = share_ref[...]
    rows = iota((all_bins, elements), 0)
    mixing = jnp.zeros((all_bins, elements), jnp.float32)
    for peak in range(peaks):
        mixing = mixing + jnp.where(
            rows == bins[peak : peak + 1, :], share[peak : peak + 1, :], 0.0
        )

    def transposed_product(values):
        return lax.dot_general(
            mixing, values, (((0,), (0,)), ((), ())), precision=HIGHEST,
            preferred_element_type=jnp.float32,
        )

    left = transposed_product(mixing)
    full = (all_bins, all_bins)
    mixing_t = transposed_product(jnp.where(iota(full, 0) == iota(full, 1), 1.0, 0.0))
    square = (elements, elements)
    left = left + jnp.where(iota(square, 0) == iota(square, 1), RIDGE_WEIGHT, 0.0)
    right = mixing_t
    for step in range(elements):
        inverse = 1.0 / left[step : step + 1, step : step + 1]
        left_row = left[step : step + 1, :] * inverse
        right_row = right[step : step + 1, :] * inverse
        column = left[:, step : step + 1]
        here = iota((elements, 1), 0) == step
        left = jnp.where(here, left_row, left - column * left_row)
        right = jnp.where(here, right_row, right - column * right_row)
    return right


def position(axis):
    return lax.axis_index(axis)


def coordinate(at, extent):
    return (2.0 * lax.convert_element_type(at, jnp.float32) + 1.0) / float(extent) - 1.0


def split_pieces(wide):
    high = wide.astype(jnp.bfloat16)
    return high, (wide - high.astype(jnp.float32)).astype(jnp.bfloat16)


def lane_parts(depth):
    return range(depth // LANES)


def plane_of(held, row, count, stride):
    parts = [held[lane, pl.ds(row, count, stride=stride), :] for lane in range(held.shape[0])]
    return jnp.concatenate(parts, axis=1).astype(jnp.float32).astype(jnp.bfloat16)


def fill_table(table, spread, layer, targets, weights):
    elements = spread.shape[0]
    for place, target in enumerate(targets):
        factor = jnp.zeros(layer.shape, jnp.float32)
        for offset in range(TAPS):
            factor = jnp.where(layer - target + REACH == offset, tap(weights, 0, offset), factor)
        table[pl.ds(place * elements, elements), :] = spread * factor
    return split_pieces(table[...])


def product(high, low, plane):
    return jnp.dot(high, plane, preferred_element_type=jnp.float32) + jnp.dot(
        low, plane, preferred_element_type=jnp.float32
    )


def add_sums(sums, mixed, ones_y, linear_y, row, first):
    plain = mixed * ones_y[row : row + 1, :]
    tilted = mixed * linear_y[row : row + 1, :]
    if first:
        sums[0], sums[1] = plain, tilted
    else:
        sums[0] += plain
        sums[1] += tilted


def plane_moments(parts, sums, targets, elements, local_x, size_x):
    for place, target in enumerate(targets):
        x = position("gx") * local_x + target
        inside = jnp.where((x >= 0) & (x < size_x), 1.0, 0.0)
        rows = pl.ds(place * elements, elements)
        plain = sums[0, rows, :] * inside
        parts[0] = parts[0] + plain
        parts[1] = parts[1] + plain * coordinate(x, size_x)
        parts[2] = parts[2] + sums[1, rows, :] * inside
    return parts


def mix_kernel(sizes, taps_hbm, bins_hbm, share_hbm, counts_ref, main_ref, up_ref, down_ref, moments_ref,
               weights_ref, taps_ref, bins_ref, share_ref, held, table, sums, small_sem, sem):
    local_bins, local_x, local_y, depth, elements, split, all_bins, size_x, size_y = sizes
    rows_in = local_bins * local_x
    small = [
        pltpu.make_async_copy(source, target, small_sem.at[i])
        for i, (source, target) in enumerate(
            ((taps_hbm, taps_ref), (bins_hbm, bins_ref), (share_hbm, share_ref))
        )
    ]
    copies = [
        pltpu.make_async_copy(
            counts_ref.at[:, pl.ds(lane * LANES, LANES)], held.at[lane], sem.at[lane]
        )
        for lane in lane_parts(depth)
    ]
    for copy in small + copies:
        copy.start()
    for copy in small:
        copy.wait()
    weights = normalized(taps_ref)
    weights_ref[...] = weights
    unmix = unmix_rows(bins_ref, share_ref, all_bins)
    shape = (all_bins, rows_in)
    expand = jnp.where(
        iota(shape, 0) == position("mz") * local_bins + iota(shape, 1) // local_x, 1.0, 0.0
    )
    spread = jnp.dot(unmix, expand, precision=HIGHEST, preferred_element_type=jnp.float32)
    layer = iota((1, rows_in), 1) % local_x
    targets = []
    for ahead in range(split):
        owner = (position("mz") + ahead) % split
        targets += [owner * REACH + j for j in range(REACH)]
    targets += [j - REACH for j in range(REACH)] + [local_x + j for j in range(REACH)]
    high, low = fill_table(table, spread, layer, targets, weights)
    rows_y = position("gy") * local_y + iota((local_y, depth), 0)
    ones_y, linear_y = adjoint(weights, 1, rows_y, size_y)
    block = REACH * elements
    for copy in copies:
        copy.wait()
    for row in range(local_y):
        mixed = product(high, low, plane_of(held, row, rows_in, local_y))
        for ahead in range(split):
            main_ref[ahead, row] = mixed[ahead * block : (ahead + 1) * block]
        up_ref[row] = mixed[split * block : (split + 1) * block]
        down_ref[row] = mixed[(split + 1) * block :]
        add_sums(sums, mixed, ones_y, linear_y, row, row == 0)
    parts = [jnp.zeros((elements, depth), jnp.float32) for _ in range(3)]
    parts = plane_moments(parts, sums, targets, elements, local_x, size_x)
    rest = jnp.zeros((LANES - 4 * elements, depth), jnp.float32)
    stacked = jnp.concatenate([parts[0], parts[1], parts[2], parts[0], rest], axis=0)
    ones_z, linear_z = adjoint(weights, 2, iota((8, depth), 1), depth)
    profile = jnp.where(iota((8, depth), 0) == 0, ones_z, linear_z)
    products = lax.dot_general(
        profile, stacked, (((1,), (1,)), ((), ())), precision=HIGHEST,
        preferred_element_type=jnp.float32,
    )
    row = jnp.where(iota((1, LANES), 1) < 3 * elements, products[0:1], products[1:2])
    moments_ref[...] = jnp.broadcast_to(row, moments_ref.shape)


def mix(taps, bins, share, counts, sizes, peers):
    local_bins, local_x, local_y, depth, elements, split, _, _, _ = sizes
    block = REACH * elements
    rows_in = local_bins * local_x
    rows_out = (split + 2) * block
    vmem = pl.BlockSpec(memory_space=pltpu.VMEM)
    hbm = pl.BlockSpec(memory_space=pltpu.HBM)
    shapes = [(split, local_y, block, depth)] + [(local_y, block, depth)] * 2 + [(8, LANES), taps.shape]
    return pl.pallas_call(
        functools.partial(mix_kernel, sizes),
        out_shape=[jax.ShapeDtypeStruct(shape, jnp.float32) for shape in shapes],
        in_specs=[hbm] * 4,
        out_specs=[vmem] * len(shapes),
        scratch_shapes=[
            pltpu.VMEM(taps.shape, jnp.float32),
            pltpu.VMEM(bins.shape, jnp.int32),
            pltpu.VMEM(share.shape, jnp.float32),
            pltpu.VMEM((depth // LANES, rows_in * local_y, LANES), jnp.int32),
            pltpu.VMEM((rows_out, rows_in), jnp.float32),
            pltpu.VMEM((2, rows_out, depth), jnp.float32),
            pltpu.SemaphoreType.DMA((3,)),
            pltpu.SemaphoreType.DMA((depth // LANES,)),
        ],
        compiler_params=pltpu.CompilerParams(vmem_limit_bytes=12 * MIB),
        cost_estimate=pl.CostEstimate(
            flops=4 * rows_out * rows_in * local_y * depth,
            bytes_accessed=8 << 20,
            transcendentals=0,
        ),
        name="mix_bins",
    )(*[
        pltpu.with_memory_space_constraint(values, pltpu.HBM)
        for values in (taps, bins, share, counts.reshape(-1, depth))
    ])


def owner_flags(ahead, split):
    owner = (position("mz") + ahead) % split
    above = jnp.where(owner == split - 1, 1.0, 0.0)
    below = jnp.where(owner == 0, 1.0, 0.0)
    return above, below


def with_edges(main_ref, above_ref, below_ref, flags, ahead, row):
    return main_ref[ahead, row] + flags[0] * above_ref[row] + flags[1] * below_ref[row]


def rows_at(slot, block):
    return pl.ds(slot * block, block)


def add_kernel(*refs):
    total = refs[0][...]
    for ref in refs[1:-1]:
        total = total + ref[...]
    refs[-1][...] = total


def first_kernel(split, half, main_ref, above_ref, below_ref, moments_ref, other_ref, up_ref, down_ref,
                 spread_ref):
    block = main_ref.shape[2]
    total = moments_ref[...] + other_ref[...]
    spread_ref[...] = jnp.broadcast_to(total[0:1], spread_ref.shape)
    for out, pieces in ((up_ref, ((2, 0), (1, half))), (down_ref, ((2, half), (3, 0)))):
        for place, (ahead, base) in enumerate(pieces):
            flags = owner_flags(ahead, split)
            for slot in range(half):
                out[rows_at(place * half + slot, block), :] = with_edges(
                    main_ref, above_ref, below_ref, flags, ahead, base + slot
                )


def late_kernel(split, half, main_ref, above_ref, below_ref, up_ref, down_ref, gathered_ref,
                early_up, early_down, late_up, late_down, summed_ref):
    total = jnp.sum(gathered_ref[...], axis=0, keepdims=True)
    summed_ref[...] = jnp.broadcast_to(total, summed_ref.shape)
    block = main_ref.shape[2]
    for ahead, base, leaf, early, late, rim in (
        (1, 0, up_ref, early_up, late_up, 0), (3, half, down_ref, early_down, late_down, half - REACH)
    ):
        flags = owner_flags(ahead, split)
        for slot in range(half):
            value = with_edges(main_ref, above_ref, below_ref, flags, ahead, base + slot)
            value = value + leaf[rows_at(slot, block), :]
            if rim <= slot < rim + REACH:
                early[rows_at(slot - rim, block), :] = value
            else:
                late[rows_at(slot if rim else slot - REACH, block), :] = value


def own_kernel(split, half, main_ref, above_ref, below_ref, up_ref, down_ref, out_ref):
    block = main_ref.shape[2]
    flags = owner_flags(0, split)
    for row in range(2 * half):
        direct = down_ref if row < half else up_ref
        out_ref[rows_at(row, block), :] = (
            with_edges(main_ref, above_ref, below_ref, flags, 0, row)
            + direct[rows_at(half + row % half, block), :]
        )


def rim_kernel(half, block, own_ref, early_up, early_down, low_ref, high_ref):
    rim = REACH * block
    low_ref[...] = own_ref[pl.ds(0, rim), :] + early_up[...]
    high_ref[...] = own_ref[pl.ds(2 * half * block - rim, rim), :] + early_down[...]


def local_call(kernel, shapes, args, name, weight=1):
    vmem = pl.BlockSpec(memory_space=pltpu.VMEM)
    size = sum(a.size for a in args) * 4 * weight
    return pl.pallas_call(
        kernel,
        out_shape=[jax.ShapeDtypeStruct(shape, jnp.float32) for shape in shapes],
        in_specs=[vmem] * len(args),
        out_specs=[vmem] * len(shapes),
        compiler_params=pltpu.CompilerParams(vmem_limit_bytes=4 * MIB),
        cost_estimate=pl.CostEstimate(flops=size, bytes_accessed=size, transcendentals=0),
        name=name,
    )(*args)


def finish_kernel(sizes, squares, weights_ref, before_ref, after_ref, low_ref, high_ref,
                  own_ref, late_up, late_down, *rest):
    moments, (out_ref, turned, sem) = rest[:-3], rest[-3:]
    local_y, depth, elements, split, local_x, size_x, size_y = sizes
    half = local_y // 2
    block = REACH * elements
    weights = weights_ref[...]
    planes = {}
    for j in range(REACH):
        rows = rows_at(j, block)
        planes[j - REACH] = before_ref[rows, :]
        planes[local_y + j] = after_ref[rows, :]
        planes[j] = low_ref[rows, :]
        planes[local_y - REACH + j] = high_ref[rows, :]
    for row in range(REACH, local_y - REACH):
        late, slot = (late_up, row - REACH) if row < half else (late_down, row - half)
        planes[row] = own_ref[rows_at(row, block), :] + late[rows_at(slot, block), :]
    totals = moments[0][0:1]
    for other in moments[1:]:
        totals = totals + other[0:1]
    lanes = iota((elements, LANES), 1)
    rows = iota((elements, LANES), 0)
    fitted = [
        jnp.sum(jnp.where(lanes == rows + j * elements, totals, 0.0), axis=1, keepdims=True)
        / squares[j]
        for j in range(4)
    ]
    at = position("gx") * local_x + position("mz") * REACH
    base = jnp.concatenate(
        [fitted[0] + fitted[1] * coordinate(at + j, size_x) for j in range(REACH)], axis=0
    )
    slope_y = jnp.concatenate([fitted[2]] * REACH, axis=0)
    slope_z = jnp.concatenate([fitted[3]] * REACH, axis=0)
    line = iota((1, depth), 1)
    tilted = base + slope_z * coordinate(line, depth)
    edge = []
    for offset in range(TAPS):
        source = line + (offset - REACH)
        edge.append(jnp.where((source >= 0) & (source < depth), tap(weights, 2, offset), 0.0))
    copies = []
    for row in range(local_y):
        smooth = tap(weights, 1, 0) * planes[row - REACH]
        for offset in range(1, TAPS):
            smooth = smooth + tap(weights, 1, offset) * planes[row + offset - REACH]
        result = -(tilted + slope_y * coordinate(position("gy") * local_y + row, size_y))
        for offset in range(TAPS):
            shifted = smooth if offset == REACH else pltpu.roll(smooth, (REACH - offset) % depth, 1)
            result = result + edge[offset] * shifted
        for j in range(REACH):
            for lane in lane_parts(depth):
                turned[lane, pl.ds(j * local_y + row, elements, stride=REACH * local_y), :] = result[
                    j * elements : (j + 1) * elements, lane * LANES : (lane + 1) * LANES
                ]
        if row % 8 == 7:
            rows = pl.ds(row - 7, 8)
            for lane in lane_parts(depth):
                source = turned.at[lane].reshape(elements * REACH, local_y, LANES)
                copy = pltpu.make_async_copy(
                    source.at[:, rows, :],
                    out_ref.at[:, rows, pl.ds(lane * LANES, LANES)],
                    sem.at[row // 8, lane],
                )
                copy.start()
                copies.append(copy)
    for copy in copies:
        copy.wait()


def finish(weights, args, sizes, squares):
    local_y, depth, elements = sizes[:3]
    vmem = pl.BlockSpec(memory_space=pltpu.VMEM)
    hbm = pl.BlockSpec(memory_space=pltpu.HBM)
    rows = elements * REACH * local_y
    return pl.pallas_call(
        functools.partial(finish_kernel, sizes, squares),
        out_shape=jax.ShapeDtypeStruct((elements * REACH, local_y, depth), jnp.float32),
        in_specs=[vmem] * (1 + len(args)),
        out_specs=hbm,
        scratch_shapes=[
            pltpu.VMEM((depth // LANES, rows, LANES), jnp.float32),
            pltpu.SemaphoreType.DMA((local_y // 8, depth // LANES)),
        ],
        compiler_params=pltpu.CompilerParams(vmem_limit_bytes=8 * MIB),
        cost_estimate=pl.CostEstimate(
            flops=30 * rows * depth, bytes_accessed=4 << 20, transcendentals=0
        ),
        name="finish",
    )(weights, *args)


def shift(values, axis, by):
    count = lax.axis_size(axis)
    return lax.ppermute(
        values, axis, [(i, i + by) for i in range(count) if 0 <= i + by < count]
    )


def turn(values, axis, by):
    count = lax.axis_size(axis)
    return lax.ppermute(values, axis, [(i, (i + by) % count) for i in range(count)])


def swap(values, axis, bit):
    return lax.ppermute(values, axis, [(i, i ^ bit) for i in range(lax.axis_size(axis))])


def squared_norms(size_x, size_y, size_z):
    def of(extent):
        return sum(((2.0 * i + 1.0) / extent - 1.0) ** 2 for i in range(extent))

    return (
        float(size_x * size_y * size_z),
        of(size_x) * size_y * size_z,
        of(size_y) * size_x * size_z,
        of(size_z) * size_x * size_y,
    )


def shards(counts, kernel_taps, peak_bins, peak_share):
    local_bins, local_x, local_y, depth = counts.shape
    elements = peak_bins.shape[0]
    split = lax.axis_size("mz")
    across = lax.axis_size("gx")
    along = lax.axis_size("gy")
    size_x = local_x * across
    size_y = local_y * along
    half = local_y // 2
    block = REACH * elements
    sizes = (local_bins, local_x, local_y, depth, elements, split, local_bins * split, size_x, size_y)
    tile = (8, LANES)
    main, up, down, moments, weights = mix(
        kernel_taps, peak_bins.T, peak_share.T, counts, sizes, across * split
    )
    from_above = shift(up, "gx", -1)
    from_below = shift(down, "gx", 1)
    for axis, by in (("gx", 1), ("mz", 1)):
        (moments,) = local_call(add_kernel, [tile], (moments, swap(moments, axis, by)), "add_sums")
    blocks = (main, from_above, from_below)
    both = (2 * half * block, depth)
    whole = (half * block, depth)
    up, down, spread = local_call(
        functools.partial(first_kernel, split, half), [both, both, (along, LANES)],
        blocks + (moments, swap(moments, "mz", 2)), "first_blocks",
    )
    up = turn(up, "mz", 1)
    down = turn(down, "mz", -1)
    gathered = lax.all_to_all(spread, "gy", 0, 0, tiled=True)
    rim = (REACH * block, depth)
    inner = ((half - REACH) * block, depth)
    early_up, early_down, late_up, late_down, moments = local_call(
        functools.partial(late_kernel, split, half), [rim, rim, inner, inner, tile],
        blocks + (up, down, gathered), "late_blocks",
    )
    early_up = turn(early_up, "mz", 1)
    early_down = turn(early_down, "mz", -1)
    late_up = turn(late_up, "mz", 1)
    late_down = turn(late_down, "mz", -1)
    (own,) = local_call(
        functools.partial(own_kernel, split, half), [(local_y * block, depth)],
        blocks + (up, down), "own_blocks",
    )
    low, high = local_call(
        functools.partial(rim_kernel, half, block), [rim, rim], (own, early_up, early_down), "rim_blocks"
    )
    before = shift(high, "gy", 1)
    after = shift(low, "gy", -1)
    result = finish(
        weights,
        (before, after, low, high, own, late_up, late_down, moments, swap(moments, "gx", 2)),
        (local_y, depth, elements, split, local_x, size_x, size_y),
        squared_norms(size_x, size_y, depth),
    )
    return result.reshape(elements, local_x // split, local_y, depth)


def solution(mesh):
    return jax.shard_map(
        shards,
        mesh=mesh,
        in_specs=(P("mz", "gx", "gy", None), P(), P(), P()),
        out_specs=P(None, ("gx", "mz"), "gy", None),
        check_vma=False,
    )
```

```python
import functools

import jax
import jax.numpy as jnp
from jax import lax
from jax.experimental import pallas as pl
from jax.experimental.pallas import tpu as pltpu
from jax.sharding import PartitionSpec as P

RIDGE_WEIGHT = 0.5
TAPS = 5
REACH = 2
LANES = 128
HIGHEST = lax.Precision.HIGHEST
MIB = 1024 * 1024
MOVED = 3

def iota(shape, dim):
    return lax.broadcasted_iota(jnp.int32, shape, dim)


def normalized(taps_ref):
    taps = taps_ref[...]
    return taps / jnp.sum(taps, axis=1, keepdims=True)


def tap(weights, axis, offset):
    return weights[axis : axis + 1, offset : offset + 1]


def adjoint(weights, axis, positions, extent):
    ones = jnp.zeros(positions.shape, jnp.float32)
    linear = jnp.zeros(positions.shape, jnp.float32)
    for offset in range(TAPS):
        target = positions - (offset - REACH)
        inside = (target >= 0) & (target < extent)
        weight = jnp.where(inside, tap(weights, axis, offset), 0.0)
        coordinate = (2.0 * target.astype(jnp.float32) + 1.0) / float(extent) - 1.0
        ones = ones + weight
        linear = linear + weight * coordinate
    return ones, linear


def unmix_rows(bins_ref, share_ref, all_bins):
    peaks, elements = bins_ref.shape
    bins = bins_ref[...]
    share = share_ref[...]
    rows = iota((all_bins, elements), 0)
    mixing = jnp.zeros((all_bins, elements), jnp.float32)
    for peak in range(peaks):
        mixing = mixing + jnp.where(
            rows == bins[peak : peak + 1, :], share[peak : peak + 1, :], 0.0
        )

    def transposed_product(values):
        return lax.dot_general(
            mixing, values, (((0,), (0,)), ((), ())), precision=HIGHEST,
            preferred_element_type=jnp.float32,
        )

    left = transposed_product(mixing)
    full = (all_bins, all_bins)
    mixing_t = transposed_product(jnp.where(iota(full, 0) == iota(full, 1), 1.0, 0.0))
    square = (elements, elements)
    left = left + jnp.where(iota(square, 0) == iota(square, 1), RIDGE_WEIGHT, 0.0)
    right = mixing_t
    for step in range(elements):
        inverse = 1.0 / left[step : step + 1, step : step + 1]
        left_row = left[step : step + 1, :] * inverse
        right_row = right[step : step + 1, :] * inverse
        column = left[:, step : step + 1]
        here = iota((elements, 1), 0) == step
        left = jnp.where(here, left_row, left - column * left_row)
        right = jnp.where(here, right_row, right - column * right_row)
    return right


def position(axis):
    return lax.axis_index(axis)


def coordinate(at, extent):
    return (2.0 * lax.convert_element_type(at, jnp.float32) + 1.0) / float(extent) - 1.0


def split_pieces(wide):
    high = wide.astype(jnp.bfloat16)
    return high, (wide - high.astype(jnp.float32)).astype(jnp.bfloat16)


def lane_parts(depth):
    return range(depth // LANES)


def plane_of(held, row, count, stride):
    parts = [held[lane, pl.ds(row, count, stride=stride), :] for lane in range(held.shape[0])]
    return jnp.concatenate(parts, axis=1).astype(jnp.float32).astype(jnp.bfloat16)


def fill_table(table, spread, layer, targets, weights):
    elements = spread.shape[0]
    for place, target in enumerate(targets):
        factor = jnp.zeros(layer.shape, jnp.float32)
        for offset in range(TAPS):
            factor = jnp.where(layer - target + REACH == offset, tap(weights, 0, offset), factor)
        table[pl.ds(place * elements, elements), :] = spread * factor
    return split_pieces(table[...])


def product(high, low, plane):
    return jnp.dot(high, plane, preferred_element_type=jnp.float32) + jnp.dot(
        low, plane, preferred_element_type=jnp.float32
    )


def add_sums(sums, mixed, ones_y, linear_y, row, first):
    plain = mixed * ones_y[row : row + 1, :]
    tilted = mixed * linear_y[row : row + 1, :]
    if first:
        sums[0], sums[1] = plain, tilted
    else:
        sums[0] += plain
        sums[1] += tilted


def plane_moments(parts, sums, targets, elements, local_x, size_x):
    for place, target in enumerate(targets):
        x = position("gx") * local_x + target
        inside = jnp.where((x >= 0) & (x < size_x), 1.0, 0.0)
        rows = pl.ds(place * elements, elements)
        plain = sums[0, rows, :] * inside
        parts[0] = parts[0] + plain
        parts[1] = parts[1] + plain * coordinate(x, size_x)
        parts[2] = parts[2] + sums[1, rows, :] * inside
    return parts


def mix_kernel(sizes, taps_hbm, bins_hbm, share_hbm, counts_ref, main_ref, up_ref, down_ref, moments_ref,
               weights_ref, taps_ref, bins_ref, share_ref, held, table, sums, small_sem, sem):
    local_bins, local_x, local_y, depth, elements, split, all_bins, size_x, size_y = sizes
    rows_in = local_bins * local_x
    small = [
        pltpu.make_async_copy(source, target, small_sem.at[i])
        for i, (source, target) in enumerate(
            ((taps_hbm, taps_ref), (bins_hbm, bins_ref), (share_hbm, share_ref))
        )
    ]
    copies = [
        pltpu.make_async_copy(
            counts_ref.at[:, pl.ds(lane * LANES, LANES)], held.at[lane], sem.at[lane]
        )
        for lane in lane_parts(depth)
    ]
    for copy in small + copies:
        copy.start()
    for copy in small:
        copy.wait()
    weights = normalized(taps_ref)
    weights_ref[...] = weights
    unmix = unmix_rows(bins_ref, share_ref, all_bins)
    shape = (all_bins, rows_in)
    expand = jnp.where(
        iota(shape, 0) == position("mz") * local_bins + iota(shape, 1) // local_x, 1.0, 0.0
    )
    spread = jnp.dot(unmix, expand, precision=HIGHEST, preferred_element_type=jnp.float32)
    layer = iota((1, rows_in), 1) % local_x
    targets = []
    for ahead in range(split):
        owner = (position("mz") + ahead) % split
        targets += [owner * REACH + j for j in range(REACH)]
    targets += [j - REACH for j in range(REACH)] + [local_x + j for j in range(REACH)]
    high, low = fill_table(table, spread, layer, targets, weights)
    rows_y = position("gy") * local_y + iota((local_y, depth), 0)
    ones_y, linear_y = adjoint(weights, 1, rows_y, size_y)
    block = REACH * elements
    for copy in copies:
        copy.wait()
    for row in range(local_y):
        mixed = product(high, low, plane_of(held, row, rows_in, local_y))
        for ahead in range(split):
            main_ref[ahead, row] = mixed[ahead * block : (ahead + 1) * block]
        up_ref[row] = mixed[split * block : (split + 1) * block]
        down_ref[row] = mixed[(split + 1) * block :]
        add_sums(sums, mixed, ones_y, linear_y, row, row == 0)
    parts = [jnp.zeros((elements, depth), jnp.float32) for _ in range(3)]
    parts = plane_moments(parts, sums, targets, elements, local_x, size_x)
    rest = jnp.zeros((LANES - 4 * elements, depth), jnp.float32)
    stacked = jnp.concatenate([parts[0], parts[1], parts[2], parts[0], rest], axis=0)
    ones_z, linear_z = adjoint(weights, 2, iota((8, depth), 1), depth)
    profile = jnp.where(iota((8, depth), 0) == 0, ones_z, linear_z)
    products = lax.dot_general(
        profile, stacked, (((1,), (1,)), ((), ())), precision=HIGHEST,
        preferred_element_type=jnp.float32,
    )
    row = jnp.where(iota((1, LANES), 1) < 3 * elements, products[0:1], products[1:2])
    moments_ref[...] = jnp.broadcast_to(row, moments_ref.shape)


def mix(taps, bins, share, counts, sizes, peers):
    local_bins, local_x, local_y, depth, elements, split, _, _, _ = sizes
    block = REACH * elements
    rows_in = local_bins * local_x
    rows_out = (split + 2) * block
    vmem = pl.BlockSpec(memory_space=pltpu.VMEM)
    hbm = pl.BlockSpec(memory_space=pltpu.HBM)
    shapes = [(split, local_y, block, depth)] + [(local_y, block, depth)] * 2 + [(8, LANES), taps.shape]
    return pl.pallas_call(
        functools.partial(mix_kernel, sizes),
        out_shape=[jax.ShapeDtypeStruct(shape, jnp.float32) for shape in shapes],
        in_specs=[hbm] * 4,
        out_specs=[vmem] * len(shapes),
        scratch_shapes=[
            pltpu.VMEM(taps.shape, jnp.float32),
            pltpu.VMEM(bins.shape, jnp.int32),
            pltpu.VMEM(share.shape, jnp.float32),
            pltpu.VMEM((depth // LANES, rows_in * local_y, LANES), jnp.int32),
            pltpu.VMEM((rows_out, rows_in), jnp.float32),
            pltpu.VMEM((2, rows_out, depth), jnp.float32),
            pltpu.SemaphoreType.DMA((3,)),
            pltpu.SemaphoreType.DMA((depth // LANES,)),
        ],
        compiler_params=pltpu.CompilerParams(vmem_limit_bytes=12 * MIB),
        cost_estimate=pl.CostEstimate(
            flops=4 * rows_out * rows_in * local_y * depth,
            bytes_accessed=8 << 20,
            transcendentals=0,
        ),
        name="mix_bins",
    )(*[
        pltpu.with_memory_space_constraint(values, pltpu.HBM)
        for values in (taps, bins, share, counts.reshape(-1, depth))
    ])


def owner_flags(ahead, split):
    owner = (position("mz") + ahead) % split
    above = jnp.where(owner == split - 1, 1.0, 0.0)
    below = jnp.where(owner == 0, 1.0, 0.0)
    return above, below


def with_edges(main_ref, above_ref, below_ref, flags, ahead, row):
    return main_ref[ahead, row] + flags[0] * above_ref[row] + flags[1] * below_ref[row]


def rows_at(slot, block):
    return pl.ds(slot * block, block)


def add_kernel(*refs):
    total = refs[0][...]
    for ref in refs[1:-1]:
        total = total + ref[...]
    refs[-1][...] = total


def first_kernel(split, half, moved, main_ref, above_ref, below_ref, moments_ref, other_ref, up_ref, down_ref,
                 across_ref, spread_ref):
    block = main_ref.shape[2]
    total = moments_ref[...] + other_ref[...]
    spread_ref[...] = jnp.broadcast_to(total[0:1], spread_ref.shape)
    inner = half - REACH
    stay = half - moved
    passed = owner_flags(2, split)
    for out, leaf, ahead, start, rim in (
        (up_ref, REACH, 1, half + moved, 0), (down_ref, half, 3, 0, half + inner)
    ):
        flags = owner_flags(ahead, split)
        rows = [(2, leaf + slot) for slot in range(inner)]
        rows += [(ahead, start + slot) for slot in range(stay)]
        rows += [(ahead, rim + slot) for slot in range(REACH)]
        for place, (part, row) in enumerate(rows):
            chosen = passed if part == 2 else flags
            out[rows_at(place, block), :] = with_edges(
                main_ref, above_ref, below_ref, chosen, part, row
            )
    for slot in range(REACH):
        for side, row in ((0, slot), (1, half + inner + slot)):
            across_ref[rows_at(side * REACH + slot, block), :] = with_edges(
                main_ref, above_ref, below_ref, passed, 2, row
            )


def late_kernel(split, half, moved, main_ref, above_ref, below_ref, up_ref, down_ref, across_ref,
                gathered_ref, late_up, late_down, own_ref, low_ref, high_ref, summed_ref):
    total = jnp.sum(gathered_ref[...], axis=0, keepdims=True)
    summed_ref[...] = jnp.broadcast_to(total, summed_ref.shape)
    block = main_ref.shape[2]
    inner = half - REACH
    for ahead, base, leaf, late, start in (
        (1, REACH, up_ref, late_up, half), (3, half, down_ref, late_down, half - moved)
    ):
        flags = owner_flags(ahead, split)
        for slot in range(inner):
            rows = rows_at(slot, block)
            value = with_edges(main_ref, above_ref, below_ref, flags, ahead, base + slot)
            late[rows, :] = value + leaf[rows, :]
        for slot in range(moved):
            late[rows_at(inner + slot, block), :] = with_edges(
                main_ref, above_ref, below_ref, flags, ahead, start + slot
            )
    own_part(split, half, moved, main_ref, above_ref, below_ref, up_ref, down_ref, across_ref,
             own_ref, low_ref, high_ref)


def own_part(split, half, moved, main_ref, above_ref, below_ref, up_ref, down_ref, across_ref,
             out_ref, low_ref, high_ref):
    block = main_ref.shape[2]
    flags = owner_flags(0, split)
    inner = half - REACH
    stay = half - moved
    for row in range(2 * half):
        value = with_edges(main_ref, above_ref, below_ref, flags, 0, row)
        if row < stay:
            value = value + down_ref[rows_at(inner + row, block), :]
        if row >= half + moved:
            value = value + up_ref[rows_at(inner + row - half - moved, block), :]
        if row < REACH:
            value = value + up_ref[rows_at(inner + stay + row, block), :]
            value = value + across_ref[rows_at(row, block), :]
            low_ref[rows_at(row, block), :] = value
        slot = row - half - inner
        if slot >= 0:
            value = value + down_ref[rows_at(inner + stay + slot, block), :]
            value = value + across_ref[rows_at(REACH + slot, block), :]
            high_ref[rows_at(slot, block), :] = value
        out_ref[rows_at(row, block), :] = value


def local_call(kernel, shapes, args, name, weight=1):
    vmem = pl.BlockSpec(memory_space=pltpu.VMEM)
    size = sum(a.size for a in args) * 4 * weight
    return pl.pallas_call(
        kernel,
        out_shape=[jax.ShapeDtypeStruct(shape, jnp.float32) for shape in shapes],
        in_specs=[vmem] * len(args),
        out_specs=[vmem] * len(shapes),
        compiler_params=pltpu.CompilerParams(vmem_limit_bytes=4 * MIB),
        cost_estimate=pl.CostEstimate(flops=size, bytes_accessed=size, transcendentals=0),
        name=name,
    )(*args)


def finish_kernel(sizes, squares, weights_ref, before_ref, after_ref, low_ref, high_ref,
                  own_ref, late_up, late_down, *rest):
    moments, (out_ref, turned, sem) = rest[:-3], rest[-3:]
    local_y, depth, elements, split, local_x, size_x, size_y, moved = sizes
    half = local_y // 2
    block = REACH * elements
    weights = weights_ref[...]
    planes = {}
    for j in range(REACH):
        rows = rows_at(j, block)
        planes[j - REACH] = before_ref[rows, :]
        planes[local_y + j] = after_ref[rows, :]
        planes[j] = low_ref[rows, :]
        planes[local_y - REACH + j] = high_ref[rows, :]
    for row in range(REACH, local_y - REACH):
        late, slot = (late_up, row - REACH) if row < half else (late_down, row - half)
        planes[row] = own_ref[rows_at(row, block), :] + late[rows_at(slot, block), :]
        if half - moved <= row < half:
            extra = rows_at(half - REACH + row - (half - moved), block)
            planes[row] = planes[row] + late_down[extra, :]
        elif half <= row < half + moved:
            planes[row] = planes[row] + late_up[rows_at(half - REACH + row - half, block), :]
    totals = moments[0][0:1]
    for other in moments[1:]:
        totals = totals + other[0:1]
    lanes = iota((elements, LANES), 1)
    rows = iota((elements, LANES), 0)
    fitted = [
        jnp.sum(jnp.where(lanes == rows + j * elements, totals, 0.0), axis=1, keepdims=True)
        / squares[j]
        for j in range(4)
    ]
    at = position("gx") * local_x + position("mz") * REACH
    base = jnp.concatenate(
        [fitted[0] + fitted[1] * coordinate(at + j, size_x) for j in range(REACH)], axis=0
    )
    slope_y = jnp.concatenate([fitted[2]] * REACH, axis=0)
    slope_z = jnp.concatenate([fitted[3]] * REACH, axis=0)
    line = iota((1, depth), 1)
    tilted = base + slope_z * coordinate(line, depth)
    edge = []
    for offset in range(TAPS):
        source = line + (offset - REACH)
        edge.append(jnp.where((source >= 0) & (source < depth), tap(weights, 2, offset), 0.0))
    copies = []
    for row in range(local_y):
        smooth = tap(weights, 1, 0) * planes[row - REACH]
        for offset in range(1, TAPS):
            smooth = smooth + tap(weights, 1, offset) * planes[row + offset - REACH]
        result = -(tilted + slope_y * coordinate(position("gy") * local_y + row, size_y))
        for offset in range(TAPS):
            shifted = smooth if offset == REACH else pltpu.roll(smooth, (REACH - offset) % depth, 1)
            result = result + edge[offset] * shifted
        for j in range(REACH):
            for lane in lane_parts(depth):
                turned[lane, pl.ds(j * local_y + row, elements, stride=REACH * local_y), :] = result[
                    j * elements : (j + 1) * elements, lane * LANES : (lane + 1) * LANES
                ]
        if row % 8 == 7:
            rows = pl.ds(row - 7, 8)
            for lane in lane_parts(depth):
                source = turned.at[lane].reshape(elements * REACH, local_y, LANES)
                copy = pltpu.make_async_copy(
                    source.at[:, rows, :],
                    out_ref.at[:, rows, pl.ds(lane * LANES, LANES)],
                    sem.at[row // 8, lane],
                )
                copy.start()
                copies.append(copy)
    for copy in copies:
        copy.wait()


def finish(weights, args, sizes, squares):
    local_y, depth, elements = sizes[:3]
    vmem = pl.BlockSpec(memory_space=pltpu.VMEM)
    hbm = pl.BlockSpec(memory_space=pltpu.HBM)
    rows = elements * REACH * local_y
    return pl.pallas_call(
        functools.partial(finish_kernel, sizes, squares),
        out_shape=jax.ShapeDtypeStruct((elements * REACH, local_y, depth), jnp.float32),
        in_specs=[vmem] * (1 + len(args)),
        out_specs=hbm,
        scratch_shapes=[
            pltpu.VMEM((depth // LANES, rows, LANES), jnp.float32),
            pltpu.SemaphoreType.DMA((local_y // 8, depth // LANES)),
        ],
        compiler_params=pltpu.CompilerParams(vmem_limit_bytes=8 * MIB),
        cost_estimate=pl.CostEstimate(
            flops=30 * rows * depth, bytes_accessed=4 << 20, transcendentals=0
        ),
        name="finish",
    )(weights, *args)


def shift(values, axis, by):
    count = lax.axis_size(axis)
    return lax.ppermute(
        values, axis, [(i, i + by) for i in range(count) if 0 <= i + by < count]
    )


def turn(values, axis, by):
    count = lax.axis_size(axis)
    return lax.ppermute(values, axis, [(i, (i + by) % count) for i in range(count)])


def swap(values, axis, bit):
    return lax.ppermute(values, axis, [(i, i ^ bit) for i in range(lax.axis_size(axis))])


def squared_norms(size_x, size_y, size_z):
    def of(extent):
        return sum(((2.0 * i + 1.0) / extent - 1.0) ** 2 for i in range(extent))

    return (
        float(size_x * size_y * size_z),
        of(size_x) * size_y * size_z,
        of(size_y) * size_x * size_z,
        of(size_z) * size_x * size_y,
    )


def shards(counts, kernel_taps, peak_bins, peak_share):
    local_bins, local_x, local_y, depth = counts.shape
    elements = peak_bins.shape[0]
    split = lax.axis_size("mz")
    across = lax.axis_size("gx")
    along = lax.axis_size("gy")
    size_x = local_x * across
    size_y = local_y * along
    half = local_y // 2
    block = REACH * elements
    sizes = (local_bins, local_x, local_y, depth, elements, split, local_bins * split, size_x, size_y)
    tile = (8, LANES)
    main, up, down, moments, weights = mix(
        kernel_taps, peak_bins.T, peak_share.T, counts, sizes, across * split
    )
    from_above = shift(up, "gx", -1)
    from_below = shift(down, "gx", 1)
    for axis, by in (("gx", 1), ("mz", 1)):
        (moments,) = local_call(add_kernel, [tile], (moments, swap(moments, axis, by)), "add_sums")
    blocks = (main, from_above, from_below)
    first = ((2 * half - MOVED) * block, depth)
    rim = (REACH * block, depth)
    second = ((half - REACH + MOVED) * block, depth)
    up, down, opposite, spread = local_call(
        functools.partial(first_kernel, split, half, MOVED),
        [first, first, (2 * REACH * block, depth), (along, LANES)],
        blocks + (moments, swap(moments, "mz", 2)), "first_blocks",
    )
    up = turn(up, "mz", 1)
    down = turn(down, "mz", -1)
    opposite = turn(opposite, "mz", 2)
    gathered = lax.all_to_all(spread, "gy", 0, 0, tiled=True)
    late_up, late_down, own, low, high, moments = local_call(
        functools.partial(late_kernel, split, half, MOVED),
        [second, second, (local_y * block, depth), rim, rim, tile],
        blocks + (up, down, opposite, gathered), "late_blocks",
    )
    late_up = turn(late_up, "mz", 1)
    late_down = turn(late_down, "mz", -1)
    before = shift(high, "gy", 1)
    after = shift(low, "gy", -1)
    result = finish(
        weights,
        (before, after, low, high, own, late_up, late_down, moments, swap(moments, "gx", 2)),
        (local_y, depth, elements, split, local_x, size_x, size_y, MOVED),
        squared_norms(size_x, size_y, depth),
    )
    return result.reshape(elements, local_x // split, local_y, depth)


def solution(mesh):
    return jax.shard_map(
        shards,
        mesh=mesh,
        in_specs=(P("mz", "gx", "gy", None), P(), P(), P()),
        out_specs=P(None, ("gx", "mz"), "gy", None),
        check_vma=False,
    )
```

```python
import functools

import jax
import jax.numpy as jnp
from jax import lax
from jax.experimental import pallas as pl
from jax.experimental.pallas import tpu as pltpu
from jax.sharding import PartitionSpec as P

RIDGE_WEIGHT = 0.5
TAPS = 5
REACH = 2
LANES = 128
HIGHEST = lax.Precision.HIGHEST
MIB = 1024 * 1024
MOVED = 3

def iota(shape, dim):
    return lax.broadcasted_iota(jnp.int32, shape, dim)


def normalized(taps_ref):
    taps = taps_ref[...]
    return taps / jnp.sum(taps, axis=1, keepdims=True)


def tap(weights, axis, offset):
    return weights[axis : axis + 1, offset : offset + 1]


def adjoint(weights, axis, positions, extent):
    ones = jnp.zeros(positions.shape, jnp.float32)
    linear = jnp.zeros(positions.shape, jnp.float32)
    for offset in range(TAPS):
        target = positions - (offset - REACH)
        inside = (target >= 0) & (target < extent)
        weight = jnp.where(inside, tap(weights, axis, offset), 0.0)
        coordinate = (2.0 * target.astype(jnp.float32) + 1.0) / float(extent) - 1.0
        ones = ones + weight
        linear = linear + weight * coordinate
    return ones, linear


def unmix_rows(bins_ref, share_ref, all_bins):
    peaks, elements = bins_ref.shape
    bins = bins_ref[...]
    share = share_ref[...]
    rows = iota((all_bins, elements), 0)
    mixing = jnp.zeros((all_bins, elements), jnp.float32)
    for peak in range(peaks):
        mixing = mixing + jnp.where(
            rows == bins[peak : peak + 1, :], share[peak : peak + 1, :], 0.0
        )

    def transposed_product(values):
        return lax.dot_general(
            mixing, values, (((0,), (0,)), ((), ())), precision=HIGHEST,
            preferred_element_type=jnp.float32,
        )

    left = transposed_product(mixing)
    full = (all_bins, all_bins)
    mixing_t = transposed_product(jnp.where(iota(full, 0) == iota(full, 1), 1.0, 0.0))
    square = (elements, elements)
    left = left + jnp.where(iota(square, 0) == iota(square, 1), RIDGE_WEIGHT, 0.0)
    right = mixing_t
    for step in range(elements):
        inverse = 1.0 / left[step : step + 1, step : step + 1]
        left_row = left[step : step + 1, :] * inverse
        right_row = right[step : step + 1, :] * inverse
        column = left[:, step : step + 1]
        here = iota((elements, 1), 0) == step
        left = jnp.where(here, left_row, left - column * left_row)
        right = jnp.where(here, right_row, right - column * right_row)
    return right


def position(axis):
    return lax.axis_index(axis)


def coordinate(at, extent):
    return (2.0 * lax.convert_element_type(at, jnp.float32) + 1.0) / float(extent) - 1.0


def split_pieces(wide):
    high = wide.astype(jnp.bfloat16)
    return high, (wide - high.astype(jnp.float32)).astype(jnp.bfloat16)


def lane_parts(depth):
    return range(depth // LANES)


def plane_of(held, row, count, stride):
    parts = [held[lane, pl.ds(row, count, stride=stride), :] for lane in range(held.shape[0])]
    return jnp.concatenate(parts, axis=1).astype(jnp.float32).astype(jnp.bfloat16)


def fill_table(table, spread, layer, targets, weights):
    elements = spread.shape[0]
    for place, target in enumerate(targets):
        factor = jnp.zeros(layer.shape, jnp.float32)
        for offset in range(TAPS):
            factor = jnp.where(layer - target + REACH == offset, tap(weights, 0, offset), factor)
        table[pl.ds(place * elements, elements), :] = spread * factor
    return split_pieces(table[...])


def product(high, low, plane):
    return jnp.dot(high, plane, preferred_element_type=jnp.float32) + jnp.dot(
        low, plane, preferred_element_type=jnp.float32
    )


def add_sums(sums, mixed, ones_y, linear_y, row, first):
    plain = mixed * ones_y[row : row + 1, :]
    tilted = mixed * linear_y[row : row + 1, :]
    if first:
        sums[0], sums[1] = plain, tilted
    else:
        sums[0] += plain
        sums[1] += tilted


def plane_moments(parts, sums, targets, elements, local_x, size_x):
    for place, target in enumerate(targets):
        x = position("gx") * local_x + target
        inside = jnp.where((x >= 0) & (x < size_x), 1.0, 0.0)
        rows = pl.ds(place * elements, elements)
        plain = sums[0, rows, :] * inside
        parts[0] = parts[0] + plain
        parts[1] = parts[1] + plain * coordinate(x, size_x)
        parts[2] = parts[2] + sums[1, rows, :] * inside
    return parts


def mix_kernel(sizes, taps_hbm, bins_hbm, share_hbm, counts_ref, main_ref, up_ref, down_ref, moments_ref,
               weights_ref, taps_ref, bins_ref, share_ref, held, table, sums, small_sem, sem):
    local_bins, local_x, local_y, depth, elements, split, all_bins, size_x, size_y = sizes
    rows_in = local_bins * local_x
    small = [
        pltpu.make_async_copy(source, target, small_sem.at[i])
        for i, (source, target) in enumerate(
            ((taps_hbm, taps_ref), (bins_hbm, bins_ref), (share_hbm, share_ref))
        )
    ]
    copies = [
        pltpu.make_async_copy(
            counts_ref.at[:, pl.ds(lane * LANES, LANES)], held.at[lane], sem.at[lane]
        )
        for lane in lane_parts(depth)
    ]
    for copy in small + copies:
        copy.start()
    for copy in small:
        copy.wait()
    weights = normalized(taps_ref)
    weights_ref[...] = weights
    unmix = unmix_rows(bins_ref, share_ref, all_bins)
    shape = (all_bins, rows_in)
    expand = jnp.where(
        iota(shape, 0) == position("mz") * local_bins + iota(shape, 1) // local_x, 1.0, 0.0
    )
    spread = jnp.dot(unmix, expand, precision=HIGHEST, preferred_element_type=jnp.float32)
    layer = iota((1, rows_in), 1) % local_x
    targets = []
    for ahead in range(split):
        owner = (position("mz") + ahead) % split
        targets += [owner * REACH + j for j in range(REACH)]
    targets += [j - REACH for j in range(REACH)] + [local_x + j for j in range(REACH)]
    high, low = fill_table(table, spread, layer, targets, weights)
    rows_y = position("gy") * local_y + iota((local_y, depth), 0)
    ones_y, linear_y = adjoint(weights, 1, rows_y, size_y)
    block = REACH * elements
    for copy in copies:
        copy.wait()
    for row in range(local_y):
        mixed = product(high, low, plane_of(held, row, rows_in, local_y))
        for ahead in range(split):
            main_ref[ahead, row] = mixed[ahead * block : (ahead + 1) * block]
        up_ref[row] = mixed[split * block : (split + 1) * block]
        down_ref[row] = mixed[(split + 1) * block :]
        add_sums(sums, mixed, ones_y, linear_y, row, row == 0)
    parts = [jnp.zeros((elements, depth), jnp.float32) for _ in range(3)]
    parts = plane_moments(parts, sums, targets, elements, local_x, size_x)
    rest = jnp.zeros((LANES - 4 * elements, depth), jnp.float32)
    stacked = jnp.concatenate([parts[0], parts[1], parts[2], parts[0], rest], axis=0)
    ones_z, linear_z = adjoint(weights, 2, iota((8, depth), 1), depth)
    profile = jnp.where(iota((8, depth), 0) == 0, ones_z, linear_z)
    products = lax.dot_general(
        profile, stacked, (((1,), (1,)), ((), ())), precision=HIGHEST,
        preferred_element_type=jnp.float32,
    )
    row = jnp.where(iota((1, LANES), 1) < 3 * elements, products[0:1], products[1:2])
    moments_ref[...] = jnp.broadcast_to(row, moments_ref.shape)


def mix(taps, bins, share, counts, sizes, peers):
    local_bins, local_x, local_y, depth, elements, split, _, _, _ = sizes
    block = REACH * elements
    rows_in = local_bins * local_x
    rows_out = (split + 2) * block
    vmem = pl.BlockSpec(memory_space=pltpu.VMEM)
    hbm = pl.BlockSpec(memory_space=pltpu.HBM)
    shapes = [(split, local_y, block, depth)] + [(local_y, block, depth)] * 2 + [(8, LANES), taps.shape]
    return pl.pallas_call(
        functools.partial(mix_kernel, sizes),
        out_shape=[jax.ShapeDtypeStruct(shape, jnp.float32) for shape in shapes],
        in_specs=[hbm] * 4,
        out_specs=[vmem] * len(shapes),
        scratch_shapes=[
            pltpu.VMEM(taps.shape, jnp.float32),
            pltpu.VMEM(bins.shape, jnp.int32),
            pltpu.VMEM(share.shape, jnp.float32),
            pltpu.VMEM((depth // LANES, rows_in * local_y, LANES), jnp.int32),
            pltpu.VMEM((rows_out, rows_in), jnp.float32),
            pltpu.VMEM((2, rows_out, depth), jnp.float32),
            pltpu.SemaphoreType.DMA((3,)),
            pltpu.SemaphoreType.DMA((depth // LANES,)),
        ],
        compiler_params=pltpu.CompilerParams(vmem_limit_bytes=12 * MIB),
        cost_estimate=pl.CostEstimate(
            flops=4 * rows_out * rows_in * local_y * depth,
            bytes_accessed=8 << 20,
            transcendentals=0,
        ),
        name="mix_bins",
    )(*[
        pltpu.with_memory_space_constraint(values, pltpu.HBM)
        for values in (taps, bins, share, counts.reshape(-1, depth))
    ])


def owner_flags(ahead, split):
    owner = (position("mz") + ahead) % split
    above = jnp.where(owner == split - 1, 1.0, 0.0)
    below = jnp.where(owner == 0, 1.0, 0.0)
    return above, below


def with_edges(main_ref, above_ref, below_ref, flags, ahead, row):
    return main_ref[ahead, row] + flags[0] * above_ref[row] + flags[1] * below_ref[row]


def rows_at(slot, block):
    return pl.ds(slot * block, block)


def add_kernel(*refs):
    total = refs[0][...]
    for ref in refs[1:-1]:
        total = total + ref[...]
    refs[-1][...] = total


def first_kernel(split, half, moved, main_ref, above_ref, below_ref, moments_ref, other_ref, up_ref, down_ref,
                 across_ref, spread_ref):
    block = main_ref.shape[2]
    total = moments_ref[...] + other_ref[...]
    spread_ref[...] = jnp.broadcast_to(total[0:1], spread_ref.shape)
    inner = half - REACH
    stay = half - moved
    passed = owner_flags(2, split)
    for out, leaf, ahead, start, rim in (
        (up_ref, REACH, 1, half + moved, 0), (down_ref, half, 3, 0, half + inner)
    ):
        flags = owner_flags(ahead, split)
        rows = [(2, leaf + slot) for slot in range(inner)]
        rows += [(ahead, start + slot) for slot in range(stay)]
        rows += [(ahead, rim + slot) for slot in range(REACH)]
        for place, (part, row) in enumerate(rows):
            chosen = passed if part == 2 else flags
            out[rows_at(place, block), :] = with_edges(
                main_ref, above_ref, below_ref, chosen, part, row
            )
    for slot in range(REACH):
        for side, row in ((0, slot), (1, half + inner + slot)):
            across_ref[rows_at(side * REACH + slot, block), :] = with_edges(
                main_ref, above_ref, below_ref, passed, 2, row
            )


def late_kernel(split, half, moved, main_ref, above_ref, below_ref, up_ref, down_ref, across_ref,
                gathered_ref, late_up, late_down, own_ref, low_ref, high_ref, summed_ref):
    total = jnp.sum(gathered_ref[...], axis=0, keepdims=True)
    summed_ref[...] = jnp.broadcast_to(total, summed_ref.shape)
    block = main_ref.shape[2]
    inner = half - REACH
    for ahead, base, leaf, late, start in (
        (1, REACH, up_ref, late_up, half), (3, half, down_ref, late_down, half - moved)
    ):
        flags = owner_flags(ahead, split)
        for slot in range(inner):
            rows = rows_at(slot, block)
            value = with_edges(main_ref, above_ref, below_ref, flags, ahead, base + slot)
            late[rows, :] = value + leaf[rows, :]
        for slot in range(moved):
            late[rows_at(inner + slot, block), :] = with_edges(
                main_ref, above_ref, below_ref, flags, ahead, start + slot
            )
    own_part(split, half, moved, main_ref, above_ref, below_ref, up_ref, down_ref, across_ref,
             own_ref, low_ref, high_ref)


def own_part(split, half, moved, main_ref, above_ref, below_ref, up_ref, down_ref, across_ref,
             out_ref, low_ref, high_ref):
    block = main_ref.shape[2]
    flags = owner_flags(0, split)
    inner = half - REACH
    stay = half - moved
    for row in range(2 * half):
        value = with_edges(main_ref, above_ref, below_ref, flags, 0, row)
        if row < stay:
            value = value + down_ref[rows_at(inner + row, block), :]
        if row >= half + moved:
            value = value + up_ref[rows_at(inner + row - half - moved, block), :]
        if row < REACH:
            value = value + up_ref[rows_at(inner + stay + row, block), :]
            value = value + across_ref[rows_at(row, block), :]
            low_ref[rows_at(row, block), :] = value
        slot = row - half - inner
        if slot >= 0:
            value = value + down_ref[rows_at(inner + stay + slot, block), :]
            value = value + across_ref[rows_at(REACH + slot, block), :]
            high_ref[rows_at(slot, block), :] = value
        out_ref[rows_at(row, block), :] = value


def local_call(kernel, shapes, args, name, weight=1):
    vmem = pl.BlockSpec(memory_space=pltpu.VMEM)
    size = sum(a.size for a in args) * 4 * weight
    return pl.pallas_call(
        kernel,
        out_shape=[jax.ShapeDtypeStruct(shape, jnp.float32) for shape in shapes],
        in_specs=[vmem] * len(args),
        out_specs=[vmem] * len(shapes),
        compiler_params=pltpu.CompilerParams(vmem_limit_bytes=4 * MIB),
        cost_estimate=pl.CostEstimate(flops=size, bytes_accessed=size, transcendentals=0),
        name=name,
    )(*args)


def finish_kernel(sizes, squares, weights_ref, before_ref, after_ref, low_ref, high_ref,
                  own_ref, late_up, late_down, *rest):
    moments, (out_ref, turned, sem) = rest[:-3], rest[-3:]
    local_y, depth, elements, split, local_x, size_x, size_y, moved = sizes
    half = local_y // 2
    block = REACH * elements
    weights = weights_ref[...]
    planes = {}
    for j in range(REACH):
        rows = rows_at(j, block)
        planes[j - REACH] = before_ref[rows, :]
        planes[local_y + j] = after_ref[rows, :]
        planes[j] = low_ref[rows, :]
        planes[local_y - REACH + j] = high_ref[rows, :]
    for row in range(REACH, local_y - REACH):
        late, slot = (late_up, row - REACH) if row < half else (late_down, row - half)
        planes[row] = own_ref[rows_at(row, block), :] + late[rows_at(slot, block), :]
        if half - moved <= row < half:
            extra = rows_at(half - REACH + row - (half - moved), block)
            planes[row] = planes[row] + late_down[extra, :]
        elif half <= row < half + moved:
            planes[row] = planes[row] + late_up[rows_at(half - REACH + row - half, block), :]
    totals = moments[0][0:1]
    for other in moments[1:]:
        totals = totals + other[0:1]
    lanes = iota((elements, LANES), 1)
    rows = iota((elements, LANES), 0)
    fitted = [
        jnp.sum(jnp.where(lanes == rows + j * elements, totals, 0.0), axis=1, keepdims=True)
        / squares[j]
        for j in range(4)
    ]
    at = position("gx") * local_x + position("mz") * REACH
    base = jnp.concatenate(
        [fitted[0] + fitted[1] * coordinate(at + j, size_x) for j in range(REACH)], axis=0
    )
    slope_y = jnp.concatenate([fitted[2]] * REACH, axis=0)
    slope_z = jnp.concatenate([fitted[3]] * REACH, axis=0)
    line = iota((1, depth), 1)
    tilted = base + slope_z * coordinate(line, depth)
    edge = []
    for offset in range(TAPS):
        source = line + (offset - REACH)
        edge.append(jnp.where((source >= 0) & (source < depth), tap(weights, 2, offset), 0.0))
    copies = []
    for row in range(local_y):
        smooth = tap(weights, 1, 0) * planes[row - REACH]
        for offset in range(1, TAPS):
            smooth = smooth + tap(weights, 1, offset) * planes[row + offset - REACH]
        result = -(tilted + slope_y * coordinate(position("gy") * local_y + row, size_y))
        for offset in range(TAPS):
            shifted = smooth if offset == REACH else pltpu.roll(smooth, (REACH - offset) % depth, 1)
            result = result + edge[offset] * shifted
        for j in range(REACH):
            for lane in lane_parts(depth):
                turned[lane, pl.ds(j * local_y + row, elements, stride=REACH * local_y), :] = result[
                    j * elements : (j + 1) * elements, lane * LANES : (lane + 1) * LANES
                ]
        if row % 8 == 7:
            rows = pl.ds(row - 7, 8)
            for lane in lane_parts(depth):
                source = turned.at[lane].reshape(elements * REACH, local_y, LANES)
                copy = pltpu.make_async_copy(
                    source.at[:, rows, :],
                    out_ref.at[:, rows, pl.ds(lane * LANES, LANES)],
                    sem.at[row // 8, lane],
                )
                copy.start()
                copies.append(copy)
    for copy in copies:
        copy.wait()


def finish(weights, args, sizes, squares):
    local_y, depth, elements = sizes[:3]
    vmem = pl.BlockSpec(memory_space=pltpu.VMEM)
    hbm = pl.BlockSpec(memory_space=pltpu.HBM)
    rows = elements * REACH * local_y
    return pl.pallas_call(
        functools.partial(finish_kernel, sizes, squares),
        out_shape=jax.ShapeDtypeStruct((elements * REACH, local_y, depth), jnp.float32),
        in_specs=[vmem] * (1 + len(args)),
        out_specs=hbm,
        scratch_shapes=[
            pltpu.VMEM((depth // LANES, rows, LANES), jnp.float32),
            pltpu.SemaphoreType.DMA((local_y // 8, depth // LANES)),
        ],
        compiler_params=pltpu.CompilerParams(vmem_limit_bytes=8 * MIB),
        cost_estimate=pl.CostEstimate(
            flops=30 * rows * depth, bytes_accessed=4 << 20, transcendentals=0
        ),
        name="finish",
    )(weights, *args)


def shift(values, axis, by):
    count = lax.axis_size(axis)
    return lax.ppermute(
        values, axis, [(i, i + by) for i in range(count) if 0 <= i + by < count]
    )


def turn(values, axis, by):
    count = lax.axis_size(axis)
    return lax.ppermute(values, axis, [(i, (i + by) % count) for i in range(count)])


def swap(values, axis, bit):
    return lax.ppermute(values, axis, [(i, i ^ bit) for i in range(lax.axis_size(axis))])


def squared_norms(size_x, size_y, size_z):
    def of(extent):
        return sum(((2.0 * i + 1.0) / extent - 1.0) ** 2 for i in range(extent))

    return (
        float(size_x * size_y * size_z),
        of(size_x) * size_y * size_z,
        of(size_y) * size_x * size_z,
        of(size_z) * size_x * size_y,
    )


def shards(counts, kernel_taps, peak_bins, peak_share):
    local_bins, local_x, local_y, depth = counts.shape
    elements = peak_bins.shape[0]
    split = lax.axis_size("mz")
    across = lax.axis_size("gx")
    along = lax.axis_size("gy")
    size_x = local_x * across
    size_y = local_y * along
    half = local_y // 2
    block = REACH * elements
    sizes = (local_bins, local_x, local_y, depth, elements, split, local_bins * split, size_x, size_y)
    tile = (8, LANES)
    main, up, down, moments, weights = mix(
        kernel_taps, peak_bins.T, peak_share.T, counts, sizes, across * split
    )
    from_above = shift(up, "gx", -1)
    from_below = shift(down, "gx", 1)
    for axis, by in (("gx", 1), ("mz", 1)):
        (moments,) = local_call(add_kernel, [tile], (moments, swap(moments, axis, by)), "add_sums")
    blocks = (main, from_above, from_below)
    first = ((2 * half - MOVED) * block, depth)
    rim = (REACH * block, depth)
    second = ((half - REACH + MOVED) * block, depth)
    up, down, opposite, spread = local_call(
        functools.partial(first_kernel, split, half, MOVED),
        [first, first, (2 * REACH * block, depth), (along, LANES)],
        blocks + (moments, swap(moments, "mz", 2)), "first_blocks",
    )
    up = turn(up, "mz", 1)
    down = turn(down, "mz", -1)
    opposite = turn(opposite, "mz", 2)
    gathered = lax.all_to_all(spread, "gy", 0, 0, tiled=True)
    late_up, late_down, own, low, high, moments = local_call(
        functools.partial(late_kernel, split, half, MOVED),
        [second, second, (local_y * block, depth), rim, rim, tile],
        blocks + (up, down, opposite, gathered), "late_blocks",
    )
    late_up = turn(late_up, "mz", 1)
    late_down = turn(late_down, "mz", -1)
    (moments,) = local_call(add_kernel, [tile], (moments, swap(moments, "gx", 2)), "add_sums")
    before = shift(high, "gy", 1)
    after = shift(low, "gy", -1)
    result = finish(
        weights,
        (before, after, low, high, own, late_up, late_down, moments),
        (local_y, depth, elements, split, local_x, size_x, size_y, MOVED),
        squared_norms(size_x, size_y, depth),
    )
    return result.reshape(elements, local_x // split, local_y, depth)


def solution(mesh):
    return jax.shard_map(
        shards,
        mesh=mesh,
        in_specs=(P("mz", "gx", "gy", None), P(), P(), P()),
        out_specs=P(None, ("gx", "mz"), "gy", None),
        check_vma=False,
    )
```
